256 devices in a mesh: band: 8 (over y, core), chan: 32 (over z, x).
Axes of the slice: x: 4, y: 4, z: 8, core: 2. Of those that a mesh axis runs over, the one named last changes fastest.
Arguments:
- spectra: bfloat16 [2, 1024, 512, 256], P(None, 'band', None, 'chan'), may hold values from -6 to 6
- exponents: int32 [1024, 512], P('band'), may hold values from -2 to 2
- counts: int32 [512], P('chan'), may hold values from 128 to 256
Outputs:
- visibilities: bfloat16 [512, 2, 1024, 1024], P('chan', None, 'band')
The draws below stay inside these ranges and needn't reach their ends.
All inputs are finite; a program needn't handle non-finite values.
Results may differ from the reference program's by a relative error of at most 0.004.
Values may be sent and summed in bfloat16 or wider, within the bound.
A program may use at most 128 MiB of HBM per device.

```python
import jax
import jax.numpy as jnp
from jax import lax

INPUTS = 1024
BLOCK = 64
CHANNELS = 512
TIME = 256


def set_ends(drawn, key, smallest, largest):
    index_at = [jax.random.randint(jax.random.fold_in(key, axis), (), 0, length) for axis, length in enumerate(drawn.shape)]
    longest = drawn.shape.index(max(drawn.shape))
    neighbour = index_at[:longest] + [(index_at[longest] + 1) % drawn.shape[longest]] + index_at[longest + 1:]
    return drawn.at[tuple(index_at)].set(smallest).at[tuple(neighbour)].set(largest)


def levels(own_key, dims, split, low, top_value):
    def one(dim, parts):
        draws = jax.random.uniform(jax.random.fold_in(jax.random.fold_in(own_key, 6), dim), (parts,), jnp.float32, low / len(split), top_value / len(split))
        return jnp.repeat(jnp.exp(draws), dims[dim] // parts).reshape((-1,) + (1,) * (len(dims) - dim - 1))

    level = one(*split[0])
    for cut in split[1:]:
        level = level * one(*cut)
    return level


def centred(own_key, extent, width, bound, split=(), held_as=jnp.bfloat16):
    drawn = width * jax.random.normal(own_key, extent, jnp.float32)
    if split:
        drawn = drawn * levels(own_key, extent, split, -0.22, 0.18)
    return jnp.clip(drawn, -bound, bound).astype(held_as)


def setup_inputs(seed: int = 0) -> dict:
    key_of = jax.random.split(jax.random.key(seed), 4)
    return {
        "spectra": centred(key_of[0], (2, INPUTS, CHANNELS, TIME), 1.0, 6.0, ((1, 8), (3, 32))),
        "exponents": set_ends(jax.random.randint(key_of[1], (INPUTS, CHANNELS), -2, 3), jax.random.fold_in(key_of[1], 1), -2, 2).astype(jnp.int32),
        "counts": set_ends(jax.random.randint(key_of[2], (CHANNELS,), TIME // 2, TIME + 1), jax.random.fold_in(key_of[2], 1), TIME // 2, TIME).astype(jnp.int32),
    }


def power_scale(exponents):
    scale = jnp.zeros(exponents.shape, jnp.float32)
    for power in range(-2, 3):
        scale = scale + jnp.where(exponents == power, jnp.float32(2.0 ** power), jnp.float32(0.0))
    return scale


def reference(spectra, exponents, counts):
    scale = power_scale(exponents)
    voltage = (spectra.astype(jnp.float32) * scale[None, :, :, None]).astype(jnp.bfloat16)
    samples = jnp.arange(TIME, dtype=jnp.int32)
    live = samples[None, :] < counts[:, None]
    voltage = jnp.where(live[None, None], voltage, jnp.zeros((), jnp.bfloat16))
    blocks = jnp.arange(INPUTS, dtype=jnp.int32) // BLOCK
    lower = (blocks[:, None] >= blocks[None, :]).astype(jnp.float32)

    def one_channel(channel):
        single = lax.dynamic_index_in_dim(voltage, channel, 2, keepdims=False)
        plain = jnp.concatenate([single[0], single[1]], axis=1)
        turned = jnp.concatenate([single[1], -single[0]], axis=1)
        real_part = jnp.dot(plain, plain.T, preferred_element_type=jnp.float32)
        imag_part = jnp.dot(turned, plain.T, preferred_element_type=jnp.float32)
        total = counts[channel].astype(jnp.float32)
        return (jnp.stack([real_part, imag_part]) * lower[None] / total).astype(jnp.bfloat16)

    return lax.map(one_channel, jnp.arange(CHANNELS, dtype=jnp.int32))
```

```python
import jax
import jax.numpy as jnp
from jax import lax
from jax.experimental import pallas as pl
from jax.experimental.pallas import tpu as pltpu
from jax.sharding import PartitionSpec as P

MESH = pl.DeviceIdType.MESH
BLOCK = 64
BANDS, CORES, YS = 8, 2, 4
ZS, XS = 8, 4
CHANS = ZS * XS
ROWS = 128
OWN = 16
SAMPLES = 8
UNIT = 2 * SAMPLES
DEPTH = CHANS * UNIT
WIDE = 2 * ROWS
GROUPS = 4
GROUP = OWN // GROUPS
EARLY = OWN - GROUP
CHUNK = 4
PARTS = CHANS // CHUNK
STEPS = GROUPS * PARTS
WHOLE = (7, 13, 20, 26)
AHEAD = 12
BY_ONE = 24
LANES = 128
SPANS = CHANS * OWN // LANES
LAG = 3
FIRST = 4
FEW = 28
FLIGHT = 4
OUT_PARTS = 6


def power_scale(exponents):
    scale = jnp.zeros(exponents.shape, jnp.float32)
    for power in range(-2, 3):
        scale = scale + jnp.where(exponents == power, jnp.float32(2.0**power), jnp.float32(0.0))
    return scale


def mod(a, n):
    return a % n if isinstance(a, int) else lax.rem(a, jnp.full_like(a, n))


def div(a, n):
    return a // n if isinstance(a, int) else lax.div(a, jnp.full_like(a, n))


def flip(a, b, bits):
    return sum(mod(div(a, 1 << n) + div(b, 1 << n), 2) * (1 << n) for n in range(bits))


def offset(k):
    return 2 * div(k, 2 * CHUNK) + mod(k, 2), div(mod(k, CHUNK), 2) + 2 * mod(div(k, CHUNK), 2)


def source(chan, k):
    dz, dx = offset(k)
    return flip(div(chan, XS), dz, 3) * XS + mod(mod(chan, XS) + dx, XS)


def target(chan, k):
    dz, dx = offset(k)
    return flip(div(chan, XS), dz, 3) * XS + mod(mod(chan, XS) + XS - dx, XS)


def lower(tile, first):
    line = lax.broadcasted_iota(jnp.int32, tile.shape, 0)
    column = lax.broadcasted_iota(jnp.int32, tile.shape, 1)
    limit = jnp.where(line < BLOCK, BLOCK, 2 * BLOCK) + first
    return jnp.where(column < limit, tile, 0.0)


def kernel(
    counts_hbm, exponents_ref, x_ref, out_ref, buf, forms, shares, counts_ref, times, powers, raw, wide, narrow, xs, load_sem,
    a2a_recv, left_recv, right_recv, relay_recv, core_recv, a2a_send, y_send, own_send, relay_send, core_send,
):
    band = lax.axis_index("band")
    chan = lax.axis_index("chan")
    y, core = div(band, CORES), mod(band, CORES)
    partner = band + 1 - 2 * core
    up, down, far = mod(y + 1, YS), mod(y + YS - 1, YS), mod(y + 2, YS)
    slow = (y == 2).astype(jnp.int32)
    relay = 9 + 3 * slow
    due_far = 14 + 3 * slow, 21 + 2 * slow, 27 + 2 * slow
    up_band, down_band, far_band = up * CORES + core, down * CORES + core, far * CORES + core

    barrier = pltpu.get_barrier_semaphore()

    def greet(k, carry):
        pl.semaphore_signal(barrier, inc=1, device_id=(band, target(chan, k)), device_id_type=MESH)
        return carry

    def drain(ref, sem):
        pltpu.make_async_copy(ref, ref, sem).wait()

    def span(n):
        return flip(div(chan, 2 * XS), n, 2)

    def lanes(n):
        return pl.ds(pl.multiple_of(span(n) * LANES, LANES), LANES)

    loads = [
        pltpu.make_async_copy(exponents_ref, powers, load_sem.at[SPANS]),
        pltpu.make_async_copy(counts_hbm, counts_ref, load_sem.at[SPANS + 1]),
    ] + [pltpu.make_async_copy(x_ref.at[:, :, lanes(n)], raw.at[n], load_sem.at[n]) for n in range(SPANS)]
    for load in loads:
        load.start()

    for other in (up_band, down_band, partner):
        pl.semaphore_signal(barrier, inc=1, device_id=(other, chan), device_id_type=MESH)
    lax.fori_loop(1, CHANS, greet, 0)

    def turn(n):
        drain(raw.at[n], load_sem.at[n])
        scale = power_scale(powers[:, lanes(n)])
        for part in range(2):
            wide[part] = raw[n, part].astype(jnp.float32)
            for t in range(SAMPLES):
                tile = wide[part, pl.ds(t, ROWS, stride=SAMPLES), :] * scale
                narrow[pl.ds(part * SAMPLES + t, LANES, stride=UNIT), :] = tile.T

        def pack(d, carry):
            own = narrow[pl.ds(pl.multiple_of(d * (OWN * UNIT), OWN * UNIT), OWN * UNIT), :]
            xs[span(n) * (LANES // OWN) + d] = own.astype(jnp.bfloat16).reshape(GROUPS, GROUP, UNIT, ROWS)
            return carry

        lax.fori_loop(0, LANES // OWN, pack, 0)

    loads[0].wait()
    turn(0)
    for g in range(GROUPS):
        pltpu.make_async_copy(xs.at[chan, g], buf.at[band, g, 0], a2a_recv.at[g * PARTS]).start()

    pl.semaphore_wait(barrier, CHANS + 2)

    def scatter(s):
        g, part = div(s, PARTS), mod(s, PARTS)

        for n in range(CHUNK):
            k = part * CHUNK + n
            to = target(chan, k)

            @pl.when(k > 0)
            def _():
                pltpu.make_async_remote_copy(
                    src_ref=xs.at[to, g], dst_ref=buf.at[band, g, k],
                    send_sem=a2a_send, recv_sem=a2a_recv.at[s],
                    device_id=(band, to), device_id_type=MESH,
                ).start()

    def scatter_all(first, end):
        def one(s, carry):
            scatter(s)
            return carry

        lax.fori_loop(first, end, one, 0)

    scatter_all(0, 2)
    turn(1)
    scatter_all(2, 4)

    piece = lax.broadcasted_iota(jnp.int32, times.shape, 0)
    row = lax.broadcasted_iota(jnp.int32, times.shape, 1)
    times[...] = source(chan, piece) * SAMPLES + mod(row, SAMPLES)
    loads[1].wait()
    for c in range(GROUP):
        shares[c] = 1.0 / jnp.full(shares.shape[1:], counts_ref[EARLY + c], jnp.int32).astype(jnp.float32)

    def chunk(of_band, s):
        g, part = div(s, PARTS), mod(s, PARTS)
        return buf.at[of_band, g, pl.ds(part * CHUNK, CHUNK)]

    def send(of_band, s, to_band, send_sem, recv_sem):
        ref = chunk(of_band, s)
        pltpu.make_async_remote_copy(
            src_ref=ref, dst_ref=ref, send_sem=send_sem, recv_sem=recv_sem,
            device_id=(to_band, chan), device_id_type=MESH,
        ).start()

    def prepare(g, c):
        slot = mod(g, 2)
        own = buf[band, g, :, c].astype(jnp.float32)
        own = jnp.where(times[...] < counts_ref[g * GROUP + c], own, 0.0)
        swapped = jnp.concatenate([own[:, SAMPLES:], -own[:, :SAMPLES]], axis=1)
        forms[slot, c, :ROWS] = own.astype(jnp.bfloat16).reshape(DEPTH, ROWS).T
        forms[slot, c, ROWS:] = swapped.astype(jnp.bfloat16).reshape(DEPTH, ROWS).T

    def gram(g, q, diagonal):
        slot = mod(g, 2)
        columns = pl.ds(pl.multiple_of(q * WIDE, WIDE), WIDE)

        for c in range(GROUP):
            right = jnp.concatenate(
                [buf[2 * q, g, :, c].reshape(DEPTH, ROWS), buf[2 * q + 1, g, :, c].reshape(DEPTH, ROWS)], axis=1
            )
            share = 1.0 / jnp.full((1, WIDE), counts_ref[g * GROUP + c], jnp.int32).astype(jnp.float32)
            product = jnp.dot(forms[slot, c], right, preferred_element_type=jnp.float32) * share
            for part in range(2):
                tile = product[part * ROWS : (part + 1) * ROWS]
                if diagonal:
                    tile = lower(tile, core * ROWS)
                out_ref[g * GROUP + c, part, :, columns] = tile.astype(jnp.bfloat16)

    def front(s, carry):
        @pl.when(s < STEPS)
        def _():
            drain(chunk(band, s), a2a_recv.at[s])

            @pl.when(y < 2)
            def _():
                send(band, s, up_band, y_send.at[0], left_recv.at[s])

            @pl.when((y == 1) & (mod(s, 2) == 1))
            def _():
                send(band, s, down_band, y_send.at[1], right_recv.at[s])

            @pl.when(core == 0)
            def _():
                send(band, s, partner, core_send.at[0], core_recv.at[0, div(s, PARTS)])

        @pl.when((s > 2) & (s < AHEAD - FIRST))
        def _():
            scatter(2 * s + FIRST)
            scatter(2 * s + FIRST + 1)

        @pl.when((s >= AHEAD - FIRST) & (s + AHEAD < STEPS))
        def _():
            scatter(s + AHEAD)

        return carry

    def pass_on(j, carry):
        @pl.when((j >= 0) & (j < STEPS) & (y == 0) & (mod(j, 2) == 1))
        def _():
            drain(chunk(up_band, j), right_recv.at[j])

            @pl.when(j >= 7)
            def _():
                drain(chunk(up_band, j - 6), relay_send.at[j - 6])

            send(up_band, j, down_band, relay_send.at[j], relay_recv.at[j])

        @pl.when((j >= 0) & (j < STEPS) & (y > 0))
        def _():
            drain(chunk(down_band, j), left_recv.at[j])

            @pl.when((y == 1) & (j >= BY_ONE))
            def _():
                send(down_band, j, up_band, y_send.at[2], relay_recv.at[j])

            @pl.when((y == 2) & (mod(j, 2) == 0))
            def _():
                @pl.when(j >= 6)
                def _():
                    drain(chunk(down_band, j - 6), relay_send.at[j - 6])

                send(down_band, j, up_band, relay_send.at[j], relay_recv.at[j])

            send(down_band, j, partner, core_send.at[1], core_recv.at[1, div(j, PARTS)])

        return carry

    def take_far(i, carry):
        @pl.when((i >= 0) & (i < STEPS))
        def _():
            drain(chunk(far_band, i), relay_recv.at[i])
            send(far_band, i, partner, core_send.at[3], core_recv.at[3, div(i, PARTS)])

        return carry

    def step(s, carry):
        def due(delay, also=None):
            late = s - delay
            ready = (late >= PARTS - 1) & (late < STEPS - PARTS) & (mod(late, PARTS) == PARTS - 1)
            return (ready if also is None else ready & also), div(late, PARTS)

        other = 1 - 2 * core

        begun = [s >= first for first in WHOLE]
        g1 = sum(one.astype(jnp.int32) for one in begun) - 1
        since = s - WHOLE[0]
        for one, first, last in zip(begun[1:], WHOLE[1:], WHOLE[:-1]):
            since = since - one.astype(jnp.int32) * (first - last)

        @pl.when((since >= 0) & (since < GROUP))
        def _():
            prepare(g1, since)

        @pl.when((since == GROUP) & (g1 < GROUPS - 1))
        def _():
            @pl.when(core == 1)
            def _():
                drain(buf.at[partner, g1], core_recv.at[0, g1])

            gram(g1, y, True)

        ready, g2 = due(LAG + 1, y > 0)

        @pl.when(ready)
        def _():
            drain(buf.at[down_band + other, g2], core_recv.at[1, g2])
            gram(g2, down, False)

        ready, g3 = due(LAG + 3, y == 3)

        @pl.when(ready)
        def _():
            drain(buf.at[up_band + other, g3], core_recv.at[2, g3])
            gram(g3, up, False)

        g4 = (s >= due_far[1]).astype(jnp.int32) + (s >= due_far[2]).astype(jnp.int32)

        @pl.when((y >= 2) & ((s == due_far[0]) | (s == due_far[1]) | (s == due_far[2])))
        def _():
            drain(buf.at[far_band + other, g4], core_recv.at[3, g4])
            gram(g4, far, False)

        begin, end = s + div(s - 1, 4), s + div(s, 4) + 1
        lax.fori_loop(begin, end, front, 0)

        @pl.when(s < 2)
        def _():
            turn(s + 2)
            scatter_all(4 + 2 * s, 6 + 4 * s)

        @pl.when((s < STEPS) & (mod(y, 2) == 0))
        def _():
            @pl.when((s >= FLIGHT) & (s < FEW))
            def _():
                drain(chunk(band, s - FLIGHT), own_send.at[s - FLIGHT])

            @pl.when(s == FEW)
            def _():
                for last in range(FEW - FLIGHT, FEW - 2):
                    drain(chunk(band, last), own_send.at[last])

            @pl.when(s >= FEW)
            def _():
                drain(chunk(band, s - 2), own_send.at[s - 2])

            @pl.when(y == 2)
            def _():
                send(band, s, up_band, own_send.at[s], left_recv.at[s])

            @pl.when(y == 0)
            def _():
                send(band, s, down_band, own_send.at[s], right_recv.at[s])

        @pl.when(y < 3)
        def _():
            lax.fori_loop(begin - LAG, end - LAG, pass_on, 0)

        j = s - LAG

        @pl.when((j >= 0) & (j < STEPS) & (y == 3))
        def _():
            drain(chunk(up_band, j), right_recv.at[j])

            @pl.when(j < BY_ONE)
            def _():
                send(up_band, j, down_band, y_send.at[2], relay_recv.at[j])

            send(up_band, j, partner, core_send.at[2], core_recv.at[2, div(j, PARTS)])
            drain(chunk(down_band, j), left_recv.at[j])
            send(down_band, j, partner, core_send.at[1], core_recv.at[1, div(j, PARTS)])

        @pl.when(y >= 2)
        def _():
            lax.fori_loop(begin - relay, end - relay, take_far, 0)

        for q in range(1, YS):

            @pl.when((s < EARLY) & (y < q))
            def _():
                out_ref[s, :, :, q * WIDE : (q + 1) * WIDE] = jnp.zeros((2, ROWS, WIDE), out_ref.dtype)

        return carry

    lax.fori_loop(0, STEPS + LAG + 1, step, 0)

    other = 1 - 2 * core
    late = GROUPS - 1

    @pl.when(core == 1)
    def _():
        drain(buf.at[partner, late], core_recv.at[0, late])

    for kind, of_band, wanted in ((1, down_band, y > 0), (2, up_band, y == 3), (3, far_band, y >= 2)):

        @pl.when(wanted)
        def _():
            drain(buf.at[of_band + other, late], core_recv.at[kind, late])

    whole = buf.at[band]
    drain(buf.at[band, :, pl.ds(0, CHANS - 1)], a2a_send)

    @pl.when(core == 0)
    def _():
        drain(whole, core_send.at[0])

    @pl.when(y < 2)
    def _():
        drain(whole, y_send.at[0])

    @pl.when(y == 1)
    def _():
        drain(xs.at[pl.ds(0, STEPS - BY_ONE)], y_send.at[2])
        drain(xs.at[pl.ds(0, STEPS // 2)], y_send.at[1])

    @pl.when(mod(y, 2) == 0)
    def _():
        for last in range(STEPS - 2, STEPS):
            drain(chunk(band, last), own_send.at[last])
        for last in (STEPS - 5, STEPS - 3, STEPS - 1):
            drain(chunk(band, 0), relay_send.at[last - div(y, 2)])

    @pl.when(y > 0)
    def _():
        drain(whole, core_send.at[1])

    @pl.when(y == 3)
    def _():
        drain(xs.at[pl.ds(0, BY_ONE)], y_send.at[2])
        drain(whole, core_send.at[2])

    @pl.when(y >= 2)
    def _():
        drain(whole, core_send.at[3])


def correlate(counts, exponents, spectra):
    dma = pltpu.SemaphoreType.DMA
    outs = (
        ((EARLY, 2, ROWS, BANDS * ROWS), jnp.bfloat16),
        ((BANDS, GROUPS, CHANS, GROUP, UNIT, ROWS), jnp.bfloat16),
        ((2, GROUP, 2 * ROWS, DEPTH), jnp.bfloat16),
        ((GROUP, 8, WIDE), jnp.float32),
    )
    return pl.pallas_call(
        kernel,
        out_shape=[pltpu.VMEM(*out) for out in outs],
        in_specs=[pl.BlockSpec(memory_space=pltpu.HBM)] * 3,
        out_specs=[pl.BlockSpec(memory_space=pltpu.VMEM)] * 4,
        scratch_shapes=[
            pltpu.SMEM((OWN,), jnp.int32),
            pltpu.VMEM((CHANS, UNIT, ROWS), jnp.int32),
            pltpu.VMEM((ROWS, CHANS * OWN), jnp.int32),
            pltpu.VMEM((SPANS, 2, ROWS * SAMPLES, LANES), jnp.bfloat16),
            pltpu.VMEM((2, ROWS * SAMPLES, LANES), jnp.float32),
            pltpu.VMEM((LANES * UNIT, ROWS), jnp.float32),
            pltpu.VMEM((CHANS, GROUPS, GROUP, UNIT, ROWS), jnp.bfloat16),
            dma((SPANS + 2,)),
            dma((STEPS,)), dma((STEPS,)), dma((STEPS,)), dma((STEPS,)), dma((4, GROUPS)),
            dma, dma((3,)), dma((STEPS,)), dma((STEPS,)), dma((4,)),
        ],
        compiler_params=pltpu.CompilerParams(
            collective_id=0, has_side_effects=True, vmem_limit_bytes=12 << 20
        ),
        name="correlate",
    )(*(pltpu.with_memory_space_constraint(operand, pltpu.HBM) for operand in (counts, exponents, spectra)))


def finish_kernel(early_ref, buf, forms, shares, out_ref, stage, early_sem, late_sem):
    band = lax.axis_index("band")
    copies = []
    for n in range(OUT_PARTS):
        part = pl.ds(n * (EARLY // OUT_PARTS), EARLY // OUT_PARTS)
        copies.append(pltpu.make_async_copy(early_ref.at[part], out_ref.at[part], early_sem.at[n]))
    for copy in copies:
        copy.start()
    late = GROUPS - 1
    for c in range(GROUP):
        for q in range(YS):
            columns = pl.ds(q * WIDE, WIDE)
            right = jnp.concatenate(
                [buf[2 * q, late, :, c].reshape(DEPTH, ROWS), buf[2 * q + 1, late, :, c].reshape(DEPTH, ROWS)], axis=1
            )
            product = jnp.dot(forms[late % 2, c], right, preferred_element_type=jnp.float32) * shares[c, :1]
            for part in range(2):
                tile = lower(product[part * ROWS : (part + 1) * ROWS], band * ROWS - q * WIDE)
                stage[c, part, :, columns] = tile.astype(jnp.bfloat16)

        copies.append(pltpu.make_async_copy(stage.at[c], out_ref.at[EARLY + c], late_sem.at[c]))
        copies[-1].start()
    for copy in copies:
        copy.wait()


def finish(early, buf, forms, shares):
    vmem = pl.BlockSpec(memory_space=pltpu.VMEM)
    return pl.pallas_call(
        finish_kernel,
        out_shape=jax.ShapeDtypeStruct((OWN, 2, ROWS, BANDS * ROWS), jnp.bfloat16),
        in_specs=[vmem] * 4,
        out_specs=pl.BlockSpec(memory_space=pl.ANY),
        scratch_shapes=[
            pltpu.VMEM((GROUP, 2, ROWS, BANDS * ROWS), jnp.bfloat16),
            pltpu.SemaphoreType.DMA((OUT_PARTS,)),
            pltpu.SemaphoreType.DMA((GROUP,)),
        ],
        compiler_params=pltpu.CompilerParams(vmem_limit_bytes=12 << 20),
        name="finish",
    )(*(pltpu.with_memory_space_constraint(operand, pltpu.VMEM) for operand in (early, buf, forms, shares)))


def local(spectra, exponents, counts):
    flat = jnp.transpose(spectra, (0, 1, 3, 2)).reshape(2, ROWS * SAMPLES, CHANS * OWN)
    return finish(*correlate(counts, exponents, flat))


def solution(mesh):
    placed = (P(None, "band", None, "chan"), P("band", None), P("chan"))
    return jax.shard_map(
        local, mesh=mesh, in_specs=placed, out_specs=P("chan", None, "band", None), check_vma=False
    )
```

```python
import jax
import jax.numpy as jnp
from jax import lax
from jax.experimental import pallas as pl
from jax.experimental.pallas import tpu as pltpu
from jax.sharding import PartitionSpec as P

MESH = pl.DeviceIdType.MESH
BLOCK = 64
BANDS, CORES, YS = 8, 2, 4
ZS, XS = 8, 4
CHANS = ZS * XS
ROWS = 128
OWN = 16
SAMPLES = 8
UNIT = 2 * SAMPLES
DEPTH = CHANS * UNIT
WIDE = 2 * ROWS
GROUPS = 4
GROUP = OWN // GROUPS
EARLY = OWN - GROUP
CHUNK = 4
PARTS = CHANS // CHUNK
STEPS = GROUPS * PARTS
WHOLE = 12, 17, 22, 27
DIRECT = 17, 23, 29
SECOND = 19, 25, 31
AHEAD = 13
BY_ONE = 24
LANES = 128
SPANS = CHANS * OWN // LANES
LAG = 3
NEAR = 2 * GROUPS
FEW = 28
FLIGHT = 4
OUT_PARTS = 6


def power_scale(exponents):
    scale = jnp.zeros(exponents.shape, jnp.float32)
    for power in range(-2, 3):
        scale = scale + jnp.where(exponents == power, jnp.float32(2.0**power), jnp.float32(0.0))
    return scale


def mod(a, n):
    return a % n if isinstance(a, int) else lax.rem(a, jnp.full_like(a, n))


def div(a, n):
    return a // n if isinstance(a, int) else lax.div(a, jnp.full_like(a, n))


def flip(a, b, bits):
    return sum(mod(div(a, 1 << n) + div(b, 1 << n), 2) * (1 << n) for n in range(bits))


def offset(k):
    return 2 * div(k, 2 * CHUNK) + mod(k, 2), div(mod(k, CHUNK), 2) + 2 * mod(div(k, CHUNK), 2)


def place(s):
    near = int(s < NEAR) if isinstance(s, int) else (s < NEAR).astype(jnp.int32)
    rest = s - NEAR
    group = near * div(s, 2) + (1 - near) * div(rest, PARTS - 2)
    return group, near * mod(s, 2) + (1 - near) * (2 + mod(rest, PARTS - 2))


def source(chan, k):
    dz, dx = offset(k)
    return flip(div(chan, XS), dz, 3) * XS + mod(mod(chan, XS) + dx, XS)


def target(chan, k):
    dz, dx = offset(k)
    return flip(div(chan, XS), dz, 3) * XS + mod(mod(chan, XS) + XS - dx, XS)


def lower(tile, first):
    line = lax.broadcasted_iota(jnp.int32, tile.shape, 0)
    column = lax.broadcasted_iota(jnp.int32, tile.shape, 1)
    limit = jnp.where(line < BLOCK, BLOCK, 2 * BLOCK) + first
    return jnp.where(column < limit, tile, 0.0)


def kernel(
    counts_hbm, exponents_ref, x_ref, out_ref, buf, forms, shares, counts_ref, times, powers, raw, wide, narrow, xs, load_sem,
    a2a_recv, left_recv, right_recv, relay_recv, core_recv, a2a_send, y_send, own_send, relay_send, core_send,
):
    band = lax.axis_index("band")
    chan = lax.axis_index("chan")
    y, core = div(band, CORES), mod(band, CORES)
    partner = band + 1 - 2 * core
    up, down, far = mod(y + 1, YS), mod(y + YS - 1, YS), mod(y + 2, YS)
    slow = (y == 2).astype(jnp.int32)
    relay = 9 + 3 * slow
    due_far = 20 + slow, 24 + 2 * slow, 30 + slow
    up_band, down_band, far_band = up * CORES + core, down * CORES + core, far * CORES + core

    barrier = pltpu.get_barrier_semaphore()

    def greet(k, carry):
        pl.semaphore_signal(barrier, inc=1, device_id=(band, target(chan, k)), device_id_type=MESH)
        return carry

    def drain(ref, sem):
        pltpu.make_async_copy(ref, ref, sem).wait()

    def span(n):
        return flip(div(chan, 2 * XS), n, 2)

    def lanes(n):
        return pl.ds(pl.multiple_of(span(n) * LANES, LANES), LANES)

    loads = [
        pltpu.make_async_copy(exponents_ref, powers, load_sem.at[SPANS]),
        pltpu.make_async_copy(counts_hbm, counts_ref, load_sem.at[SPANS + 1]),
    ] + [pltpu.make_async_copy(x_ref.at[:, :, lanes(n)], raw.at[n], load_sem.at[n]) for n in range(SPANS)]
    for load in loads:
        load.start()

    for other in (up_band, down_band, partner):
        pl.semaphore_signal(barrier, inc=1, device_id=(other, chan), device_id_type=MESH)
    lax.fori_loop(1, CHANS, greet, 0)

    def turn(n):
        drain(raw.at[n], load_sem.at[n])
        scale = power_scale(powers[:, lanes(n)])
        for part in range(2):
            wide[part] = raw[n, part].astype(jnp.float32)
            for t in range(SAMPLES):
                tile = wide[part, pl.ds(t, ROWS, stride=SAMPLES), :] * scale
                narrow[pl.ds(part * SAMPLES + t, LANES, stride=UNIT), :] = tile.T

        def pack(d, carry):
            own = narrow[pl.ds(pl.multiple_of(d * (OWN * UNIT), OWN * UNIT), OWN * UNIT), :]
            xs[span(n) * (LANES // OWN) + d] = own.astype(jnp.bfloat16).reshape(GROUPS, GROUP, UNIT, ROWS)
            return carry

        lax.fori_loop(0, LANES // OWN, pack, 0)

    loads[0].wait()
    turn(0)
    for g in range(GROUPS):
        pltpu.make_async_copy(xs.at[chan, g], buf.at[band, g, 0], a2a_recv.at[2 * g]).start()

    pl.semaphore_wait(barrier, CHANS + 2)

    def scatter(s):
        g, part = place(s)

        for n in range(CHUNK):
            k = part * CHUNK + n
            to = target(chan, k)

            @pl.when(k > 0)
            def _():
                pltpu.make_async_remote_copy(
                    src_ref=xs.at[to, g], dst_ref=buf.at[band, g, k],
                    send_sem=a2a_send, recv_sem=a2a_recv.at[s],
                    device_id=(band, to), device_id_type=MESH,
                ).start()

    def scatter_all(first, end):
        def one(s, carry):
            scatter(s)
            return carry

        lax.fori_loop(first, end, one, 0)

    scatter_all(0, NEAR // 2)

    piece = lax.broadcasted_iota(jnp.int32, times.shape, 0)
    row = lax.broadcasted_iota(jnp.int32, times.shape, 1)
    times[...] = source(chan, piece) * SAMPLES + mod(row, SAMPLES)
    loads[1].wait()
    for c in range(GROUP):
        shares[c] = 1.0 / jnp.full(shares.shape[1:], counts_ref[EARLY + c], jnp.int32).astype(jnp.float32)

    def chunk(of_band, s):
        g, part = place(s)
        return buf.at[of_band, g, pl.ds(part * CHUNK, CHUNK)]

    def send(of_band, s, to_band, send_sem, recv_sem):
        ref = chunk(of_band, s)
        pltpu.make_async_remote_copy(
            src_ref=ref, dst_ref=ref, send_sem=send_sem, recv_sem=recv_sem,
            device_id=(to_band, chan), device_id_type=MESH,
        ).start()

    def prepare(g, c):
        slot = mod(g, 2)
        own = buf[band, g, :, c].astype(jnp.float32)
        own = jnp.where(times[...] < counts_ref[g * GROUP + c], own, 0.0)
        swapped = jnp.concatenate([own[:, SAMPLES:], -own[:, :SAMPLES]], axis=1)
        forms[slot, c, :ROWS] = own.astype(jnp.bfloat16).reshape(DEPTH, ROWS).T
        forms[slot, c, ROWS:] = swapped.astype(jnp.bfloat16).reshape(DEPTH, ROWS).T

    def gram(g, q, diagonal):
        slot = mod(g, 2)
        columns = pl.ds(pl.multiple_of(q * WIDE, WIDE), WIDE)

        for c in range(GROUP):
            right = jnp.concatenate(
                [buf[2 * q, g, :, c].reshape(DEPTH, ROWS), buf[2 * q + 1, g, :, c].reshape(DEPTH, ROWS)], axis=1
            )
            share = 1.0 / jnp.full((1, WIDE), counts_ref[g * GROUP + c], jnp.int32).astype(jnp.float32)
            product = jnp.dot(forms[slot, c], right, preferred_element_type=jnp.float32) * share
            for part in range(2):
                tile = product[part * ROWS : (part + 1) * ROWS]
                if diagonal:
                    tile = lower(tile, core * ROWS)
                out_ref[g * GROUP + c, part, :, columns] = tile.astype(jnp.bfloat16)

    def front(s, carry):
        @pl.when(s < STEPS)
        def _():
            drain(chunk(band, s), a2a_recv.at[s])

            @pl.when(y < 2)
            def _():
                send(band, s, up_band, y_send.at[0], left_recv.at[s])

            @pl.when((y == 1) & (mod(s, 2) == 1))
            def _():
                send(band, s, down_band, y_send.at[1], right_recv.at[s])

            @pl.when(core == 0)
            def _():
                send(band, s, partner, core_send.at[0], core_recv.at[0, place(s)[0]])

        @pl.when((s > 2) & (s + AHEAD < STEPS))
        def _():
            scatter(s + AHEAD)

        return carry

    def pass_on(j, carry):
        @pl.when((j >= 0) & (j < STEPS) & (y == 0) & (mod(j, 2) == 1))
        def _():
            drain(chunk(up_band, j), right_recv.at[j])

            @pl.when(j >= 7)
            def _():
                drain(chunk(up_band, j - 6), relay_send.at[j - 6])

            send(up_band, j, down_band, relay_send.at[j], relay_recv.at[j])

        @pl.when((j >= 0) & (j < STEPS) & (y > 0))
        def _():
            drain(chunk(down_band, j), left_recv.at[j])

            @pl.when((y == 1) & (j >= BY_ONE))
            def _():
                send(down_band, j, up_band, y_send.at[2], relay_recv.at[j])

            @pl.when((y == 2) & (mod(j, 2) == 0))
            def _():
                @pl.when(j >= 6)
                def _():
                    drain(chunk(down_band, j - 6), relay_send.at[j - 6])

                send(down_band, j, up_band, relay_send.at[j], relay_recv.at[j])

            send(down_band, j, partner, core_send.at[1], core_recv.at[1, place(j)[0]])

        return carry

    def take_far(i, carry):
        @pl.when((i >= 0) & (i < STEPS))
        def _():
            drain(chunk(far_band, i), relay_recv.at[i])
            send(far_band, i, partner, core_send.at[3], core_recv.at[3, place(i)[0]])

        return carry

    def step(s, carry):
        def due(steps):
            ready = (s == steps[0]) | (s == steps[1]) | (s == steps[2])
            return ready, (s >= steps[1]).astype(jnp.int32) + (s >= steps[2]).astype(jnp.int32)

        other = 1 - 2 * core

        begun = [s >= first for first in WHOLE]
        g1 = sum(one.astype(jnp.int32) for one in begun) - 1
        since = s - WHOLE[0]
        for one, first, last in zip(begun[1:], WHOLE[1:], WHOLE[:-1]):
            since = since - one.astype(jnp.int32) * (first - last)

        @pl.when((since >= 0) & (since < GROUP))
        def _():
            prepare(g1, since)

        @pl.when((since == GROUP) & (g1 < GROUPS - 1))
        def _():
            @pl.when(core == 1)
            def _():
                drain(buf.at[partner, g1], core_recv.at[0, g1])

            gram(g1, y, True)

        ready, g2 = due(DIRECT)

        @pl.when(ready & (y > 0))
        def _():
            drain(buf.at[down_band + other, g2], core_recv.at[1, g2])
            gram(g2, down, False)

        ready, g3 = due(SECOND)

        @pl.when(ready & (y == 3))
        def _():
            drain(buf.at[up_band + other, g3], core_recv.at[2, g3])
            gram(g3, up, False)

        ready, g4 = due(due_far)

        @pl.when(ready & (y >= 2))
        def _():
            drain(buf.at[far_band + other, g4], core_recv.at[3, g4])
            gram(g4, far, False)

        begin, end = s + div(s - 1, 4), s + div(s, 4) + 1
        lax.fori_loop(begin, end, front, 0)

        @pl.when((s < STEPS) & (mod(y, 2) == 0))
        def _():
            @pl.when((s >= FLIGHT) & (s < FEW))
            def _():
                drain(chunk(band, s - FLIGHT), own_send.at[s - FLIGHT])

            @pl.when(s == FEW)
            def _():
                for last in range(FEW - FLIGHT, FEW - 2):
                    drain(chunk(band, last), own_send.at[last])

            @pl.when(s >= FEW)
            def _():
                drain(chunk(band, s - 2), own_send.at[s - 2])

            @pl.when(y == 2)
            def _():
                send(band, s, up_band, own_send.at[s], left_recv.at[s])

            @pl.when(y == 0)
            def _():
                send(band, s, down_band, own_send.at[s], right_recv.at[s])

        @pl.when(s == 0)
        def _():
            scatter_all(NEAR // 2, NEAR)

        @pl.when(s < SPANS - 1)
        def _():
            turn(s + 1)
            scatter_all(NEAR + 2 * s, NEAR + 2 * s + 2)

        @pl.when(s == SPANS - 2)
        def _():
            scatter_all(NEAR + 2 * SPANS - 2, AHEAD + 3)

        @pl.when(y < 3)
        def _():
            lax.fori_loop(begin - LAG, end - LAG, pass_on, 0)

        j = s - LAG

        @pl.when((j >= 0) & (j < STEPS) & (y == 3))
        def _():
            drain(chunk(up_band, j), right_recv.at[j])

            @pl.when(j < BY_ONE)
            def _():
                send(up_band, j, down_band, y_send.at[2], relay_recv.at[j])

            send(up_band, j, partner, core_send.at[2], core_recv.at[2, place(j)[0]])
            drain(chunk(down_band, j), left_recv.at[j])
            send(down_band, j, partner, core_send.at[1], core_recv.at[1, place(j)[0]])

        @pl.when(y >= 2)
        def _():
            lax.fori_loop(begin - relay, end - relay, take_far, 0)

        for q in range(1, YS):

            @pl.when((s < EARLY) & (y < q))
            def _():
                out_ref[s, :, :, q * WIDE : (q + 1) * WIDE] = jnp.zeros((2, ROWS, WIDE), out_ref.dtype)

        return carry

    lax.fori_loop(0, STEPS + LAG + 1, step, 0)

    other = 1 - 2 * core
    late = GROUPS - 1

    @pl.when(core == 1)
    def _():
        drain(buf.at[partner, late], core_recv.at[0, late])

    for kind, of_band, wanted in ((1, down_band, y > 0), (2, up_band, y == 3), (3, far_band, y >= 2)):

        @pl.when(wanted)
        def _():
            drain(buf.at[of_band + other, late], core_recv.at[kind, late])

    whole = buf.at[band]
    drain(buf.at[band, :, pl.ds(0, CHANS - 1)], a2a_send)

    @pl.when(core == 0)
    def _():
        drain(whole, core_send.at[0])

    @pl.when(y < 2)
    def _():
        drain(whole, y_send.at[0])

    @pl.when(y == 1)
    def _():
        drain(xs.at[pl.ds(0, STEPS - BY_ONE)], y_send.at[2])
        drain(xs.at[pl.ds(0, STEPS // 2)], y_send.at[1])

    @pl.when(mod(y, 2) == 0)
    def _():
        for last in range(STEPS - 2, STEPS):
            drain(chunk(band, last), own_send.at[last])
        for last in (STEPS - 5, STEPS - 3, STEPS - 1):
            drain(chunk(band, 0), relay_send.at[last - div(y, 2)])

    @pl.when(y > 0)
    def _():
        drain(whole, core_send.at[1])

    @pl.when(y == 3)
    def _():
        drain(xs.at[pl.ds(0, BY_ONE)], y_send.at[2])
        drain(whole, core_send.at[2])

    @pl.when(y >= 2)
    def _():
        drain(whole, core_send.at[3])


def correlate(counts, exponents, spectra):
    dma = pltpu.SemaphoreType.DMA
    outs = (
        ((EARLY, 2, ROWS, BANDS * ROWS), jnp.bfloat16),
        ((BANDS, GROUPS, CHANS, GROUP, UNIT, ROWS), jnp.bfloat16),
        ((2, GROUP, 2 * ROWS, DEPTH), jnp.bfloat16),
        ((GROUP, 8, WIDE), jnp.float32),
    )
    return pl.pallas_call(
        kernel,
        out_shape=[pltpu.VMEM(*out) for out in outs],
        in_specs=[pl.BlockSpec(memory_space=pltpu.HBM)] * 3,
        out_specs=[pl.BlockSpec(memory_space=pltpu.VMEM)] * 4,
        scratch_shapes=[
            pltpu.SMEM((OWN,), jnp.int32),
            pltpu.VMEM((CHANS, UNIT, ROWS), jnp.int32),
            pltpu.VMEM((ROWS, CHANS * OWN), jnp.int32),
            pltpu.VMEM((SPANS, 2, ROWS * SAMPLES, LANES), jnp.bfloat16),
            pltpu.VMEM((2, ROWS * SAMPLES, LANES), jnp.float32),
            pltpu.VMEM((LANES * UNIT, ROWS), jnp.float32),
            pltpu.VMEM((CHANS, GROUPS, GROUP, UNIT, ROWS), jnp.bfloat16),
            dma((SPANS + 2,)),
            dma((STEPS,)), dma((STEPS,)), dma((STEPS,)), dma((STEPS,)), dma((4, GROUPS)),
            dma, dma((3,)), dma((STEPS,)), dma((STEPS,)), dma((4,)),
        ],
        compiler_params=pltpu.CompilerParams(
            collective_id=0, has_side_effects=True, vmem_limit_bytes=12 << 20
        ),
        name="correlate",
    )(*(pltpu.with_memory_space_constraint(operand, pltpu.HBM) for operand in (counts, exponents, spectra)))


def finish_kernel(early_ref, buf, forms, shares, out_ref, stage, early_sem, late_sem):
    band = lax.axis_index("band")
    copies = []
    for n in range(OUT_PARTS):
        part = pl.ds(n * (EARLY // OUT_PARTS), EARLY // OUT_PARTS)
        copies.append(pltpu.make_async_copy(early_ref.at[part], out_ref.at[part], early_sem.at[n]))
    for copy in copies:
        copy.start()
    late = GROUPS - 1
    for c in range(GROUP):
        for q in range(YS):
            columns = pl.ds(q * WIDE, WIDE)
            right = jnp.concatenate(
                [buf[2 * q, late, :, c].reshape(DEPTH, ROWS), buf[2 * q + 1, late, :, c].reshape(DEPTH, ROWS)], axis=1
            )
            product = jnp.dot(forms[late % 2, c], right, preferred_element_type=jnp.float32) * shares[c, :1]
            for part in range(2):
                tile = lower(product[part * ROWS : (part + 1) * ROWS], band * ROWS - q * WIDE)
                stage[c, part, :, columns] = tile.astype(jnp.bfloat16)

        copies.append(pltpu.make_async_copy(stage.at[c], out_ref.at[EARLY + c], late_sem.at[c]))
        copies[-1].start()
    for copy in copies:
        copy.wait()


def finish(early, buf, forms, shares):
    vmem = pl.BlockSpec(memory_space=pltpu.VMEM)
    return pl.pallas_call(
        finish_kernel,
        out_shape=jax.ShapeDtypeStruct((OWN, 2, ROWS, BANDS * ROWS), jnp.bfloat16),
        in_specs=[vmem] * 4,
        out_specs=pl.BlockSpec(memory_space=pl.ANY),
        scratch_shapes=[
            pltpu.VMEM((GROUP, 2, ROWS, BANDS * ROWS), jnp.bfloat16),
            pltpu.SemaphoreType.DMA((OUT_PARTS,)),
            pltpu.SemaphoreType.DMA((GROUP,)),
        ],
        compiler_params=pltpu.CompilerParams(vmem_limit_bytes=12 << 20),
        name="finish",
    )(*(pltpu.with_memory_space_constraint(operand, pltpu.VMEM) for operand in (early, buf, forms, shares)))


def local(spectra, exponents, counts):
    flat = jnp.transpose(spectra, (0, 1, 3, 2)).reshape(2, ROWS * SAMPLES, CHANS * OWN)
    return finish(*correlate(counts, exponents, flat))


def solution(mesh):
    placed = (P(None, "band", None, "chan"), P("band", None), P("chan"))
    return jax.shard_map(
        local, mesh=mesh, in_specs=placed, out_specs=P("chan", None, "band", None), check_vma=False
    )
```

```python
import jax
import jax.numpy as jnp
from jax import lax
from jax.experimental import pallas as pl
from jax.experimental.pallas import tpu as pltpu
from jax.sharding import PartitionSpec as P

MESH = pl.DeviceIdType.MESH
BLOCK = 64
BANDS, CORES, YS = 8, 2, 4
ZS, XS = 8, 4
CHANS = ZS * XS
ROWS = 128
OWN = 16
SAMPLES = 8
UNIT = 2 * SAMPLES
DEPTH = CHANS * UNIT
WIDE = 2 * ROWS
GROUPS = 4
GROUP = OWN // GROUPS
EARLY = OWN - GROUP
CHUNK = 4
PARTS = CHANS // CHUNK
STEPS = GROUPS * PARTS
WHOLE = 12, 17, 22, 27
DIRECT = 17, 23, 29
SECOND = 19, 25, 31
AHEAD = 16
BY_ONE = 24
LANES = 128
SPANS = CHANS * OWN // LANES
LAG = 3
NEAR = 2 * GROUPS
FEW = 28
FLIGHT = 4
OUT_PARTS = 6


def power_scale(exponents):
    scale = jnp.zeros(exponents.shape, jnp.float32)
    for power in range(-2, 3):
        scale = scale + jnp.where(exponents == power, jnp.float32(2.0**power), jnp.float32(0.0))
    return scale


def mod(a, n):
    return a % n if isinstance(a, int) else lax.rem(a, jnp.full_like(a, n))


def div(a, n):
    return a // n if isinstance(a, int) else lax.div(a, jnp.full_like(a, n))


def flip(a, b, bits):
    return sum(mod(div(a, 1 << n) + div(b, 1 << n), 2) * (1 << n) for n in range(bits))


def offset(k):
    return 2 * div(k, 2 * CHUNK) + mod(k, 2), div(mod(k, CHUNK), 2) + 2 * mod(div(k, CHUNK), 2)


def place(s):
    near = int(s < NEAR) if isinstance(s, int) else (s < NEAR).astype(jnp.int32)
    rest = s - NEAR
    group = near * div(s, 2) + (1 - near) * div(rest, PARTS - 2)
    return group, near * mod(s, 2) + (1 - near) * (2 + mod(rest, PARTS - 2))


def source(chan, k):
    dz, dx = offset(k)
    return flip(div(chan, XS), dz, 3) * XS + mod(mod(chan, XS) + dx, XS)


def target(chan, k):
    dz, dx = offset(k)
    return flip(div(chan, XS), dz, 3) * XS + mod(mod(chan, XS) + XS - dx, XS)


def lower(tile, first):
    line = lax.broadcasted_iota(jnp.int32, tile.shape, 0)
    column = lax.broadcasted_iota(jnp.int32, tile.shape, 1)
    limit = jnp.where(line < BLOCK, BLOCK, 2 * BLOCK) + first
    return jnp.where(column < limit, tile, 0.0)


def kernel(
    counts_hbm, exponents_ref, x_ref, out_ref, buf, forms, shares, counts_ref, times, powers, raw, wide, narrow, xs, load_sem,
    a2a_recv, left_recv, right_recv, relay_recv, core_recv, a2a_send, y_send, own_send, relay_send, core_send,
):
    band = lax.axis_index("band")
    chan = lax.axis_index("chan")
    y, core = div(band, CORES), mod(band, CORES)
    partner = band + 1 - 2 * core
    up, down, far = mod(y + 1, YS), mod(y + YS - 1, YS), mod(y + 2, YS)
    slow = (y == 2).astype(jnp.int32)
    relay = 9 + 3 * slow
    due_far = 20 + slow, 24 + 2 * slow, 30 + slow
    up_band, down_band, far_band = up * CORES + core, down * CORES + core, far * CORES + core

    barrier = pltpu.get_barrier_semaphore()

    def greet(k, carry):
        pl.semaphore_signal(barrier, inc=1, device_id=(band, target(chan, k)), device_id_type=MESH)
        return carry

    def drain(ref, sem):
        pltpu.make_async_copy(ref, ref, sem).wait()

    def span(n):
        return flip(div(chan, 2 * XS), n, 2)

    def lanes(n):
        return pl.ds(pl.multiple_of(span(n) * LANES, LANES), LANES)

    loads = [
        pltpu.make_async_copy(exponents_ref, powers, load_sem.at[SPANS]),
        pltpu.make_async_copy(counts_hbm, counts_ref, load_sem.at[SPANS + 1]),
    ] + [pltpu.make_async_copy(x_ref.at[:, :, lanes(n)], raw.at[n], load_sem.at[n]) for n in range(SPANS)]
    for load in loads:
        load.start()

    for other in (up_band, down_band, partner):
        pl.semaphore_signal(barrier, inc=1, device_id=(other, chan), device_id_type=MESH)
    lax.fori_loop(1, CHANS, greet, 0)

    def turn(n):
        drain(raw.at[n], load_sem.at[n])
        scale = power_scale(powers[:, lanes(n)])
        for part in range(2):
            wide[part] = raw[n, part].astype(jnp.float32)
            for t in range(SAMPLES):
                tile = wide[part, pl.ds(t, ROWS, stride=SAMPLES), :] * scale
                narrow[pl.ds(part * SAMPLES + t, LANES, stride=UNIT), :] = tile.T

        def pack(d, carry):
            own = narrow[pl.ds(pl.multiple_of(d * (OWN * UNIT), OWN * UNIT), OWN * UNIT), :]
            xs[span(n) * (LANES // OWN) + d] = own.astype(jnp.bfloat16).reshape(GROUPS, GROUP, UNIT, ROWS)
            return carry

        lax.fori_loop(0, LANES // OWN, pack, 0)

    loads[0].wait()
    turn(0)
    for g in range(GROUPS):
        pltpu.make_async_copy(xs.at[chan, g], buf.at[band, g, 0], a2a_recv.at[2 * g]).start()

    pl.semaphore_wait(barrier, CHANS + 2)

    def scatter(s):
        g, part = place(s)

        for n in range(CHUNK):
            k = part * CHUNK + n
            to = target(chan, k)

            @pl.when(k > 0)
            def _():
                pltpu.make_async_remote_copy(
                    src_ref=xs.at[to, g], dst_ref=buf.at[band, g, k],
                    send_sem=a2a_send, recv_sem=a2a_recv.at[s],
                    device_id=(band, to), device_id_type=MESH,
                ).start()

    def scatter_all(first, end):
        def one(s, carry):
            scatter(s)
            return carry

        lax.fori_loop(first, end, one, 0)

    scatter_all(0, NEAR // 2)

    piece = lax.broadcasted_iota(jnp.int32, times.shape, 0)
    row = lax.broadcasted_iota(jnp.int32, times.shape, 1)
    times[...] = source(chan, piece) * SAMPLES + mod(row, SAMPLES)
    loads[1].wait()
    for c in range(GROUP):
        shares[c] = 1.0 / jnp.full(shares.shape[1:], counts_ref[EARLY + c], jnp.int32).astype(jnp.float32)

    def chunk(of_band, s):
        g, part = place(s)
        return buf.at[of_band, g, pl.ds(part * CHUNK, CHUNK)]

    def send(of_band, s, to_band, send_sem, recv_sem):
        ref = chunk(of_band, s)
        pltpu.make_async_remote_copy(
            src_ref=ref, dst_ref=ref, send_sem=send_sem, recv_sem=recv_sem,
            device_id=(to_band, chan), device_id_type=MESH,
        ).start()

    def prepare(g, c):
        slot = mod(g, 2)
        own = buf[band, g, :, c].astype(jnp.float32)
        own = jnp.where(times[...] < counts_ref[g * GROUP + c], own, 0.0)
        swapped = jnp.concatenate([own[:, SAMPLES:], -own[:, :SAMPLES]], axis=1)
        forms[slot, c, :ROWS] = own.astype(jnp.bfloat16).reshape(DEPTH, ROWS).T
        forms[slot, c, ROWS:] = swapped.astype(jnp.bfloat16).reshape(DEPTH, ROWS).T

    def gram(g, q, diagonal):
        slot = mod(g, 2)
        columns = pl.ds(pl.multiple_of(q * WIDE, WIDE), WIDE)

        for c in range(GROUP):
            right = jnp.concatenate(
                [buf[2 * q, g, :, c].reshape(DEPTH, ROWS), buf[2 * q + 1, g, :, c].reshape(DEPTH, ROWS)], axis=1
            )
            share = 1.0 / jnp.full((1, WIDE), counts_ref[g * GROUP + c], jnp.int32).astype(jnp.float32)
            product = jnp.dot(forms[slot, c], right, preferred_element_type=jnp.float32) * share
            for part in range(2):
                tile = product[part * ROWS : (part + 1) * ROWS]
                if diagonal:
                    tile = lower(tile, core * ROWS)
                out_ref[g * GROUP + c, part, :, columns] = tile.astype(jnp.bfloat16)

    def front(s, carry):
        @pl.when(s < STEPS)
        def _():
            drain(chunk(band, s), a2a_recv.at[s])

            @pl.when(y < 2)
            def _():
                send(band, s, up_band, y_send.at[0], left_recv.at[s])

            @pl.when((y == 1) & (mod(s, 2) == 1))
            def _():
                send(band, s, down_band, y_send.at[1], right_recv.at[s])

            @pl.when(core == 0)
            def _():
                send(band, s, partner, core_send.at[0], core_recv.at[0, place(s)[0]])

        @pl.when((s > 2) & (s + AHEAD < STEPS))
        def _():
            scatter(s + AHEAD)

        return carry

    def pass_on(j, carry):
        @pl.when((j >= 0) & (j < STEPS) & (y == 0) & (mod(j, 2) == 1))
        def _():
            drain(chunk(up_band, j), right_recv.at[j])

            @pl.when(j >= 7)
            def _():
                drain(chunk(up_band, j - 6), relay_send.at[j - 6])

            send(up_band, j, down_band, relay_send.at[j], relay_recv.at[j])

        @pl.when((j >= 0) & (j < STEPS) & (y > 0))
        def _():
            drain(chunk(down_band, j), left_recv.at[j])

            @pl.when((y == 1) & (j >= BY_ONE))
            def _():
                send(down_band, j, up_band, y_send.at[2], relay_recv.at[j])

            @pl.when((y == 2) & (mod(j, 2) == 0))
            def _():
                @pl.when(j >= 6)
                def _():
                    drain(chunk(down_band, j - 6), relay_send.at[j - 6])

                send(down_band, j, up_band, relay_send.at[j], relay_recv.at[j])

            send(down_band, j, partner, core_send.at[1], core_recv.at[1, place(j)[0]])

        return carry

    def take_far(i, carry):
        @pl.when((i >= 0) & (i < STEPS))
        def _():
            drain(chunk(far_band, i), relay_recv.at[i])
            send(far_band, i, partner, core_send.at[3], core_recv.at[3, place(i)[0]])

        return carry

    def step(s, carry):
        def due(steps):
            ready = (s == steps[0]) | (s == steps[1]) | (s == steps[2])
            return ready, (s >= steps[1]).astype(jnp.int32) + (s >= steps[2]).astype(jnp.int32)

        other = 1 - 2 * core

        begun = [s >= first for first in WHOLE]
        g1 = sum(one.astype(jnp.int32) for one in begun) - 1
        since = s - WHOLE[0]
        for one, first, last in zip(begun[1:], WHOLE[1:], WHOLE[:-1]):
            since = since - one.astype(jnp.int32) * (first - last)

        @pl.when((since >= 0) & (since < GROUP))
        def _():
            prepare(g1, since)

        @pl.when((since == GROUP) & (g1 < GROUPS - 1))
        def _():
            @pl.when(core == 1)
            def _():
                drain(buf.at[partner, g1], core_recv.at[0, g1])

            gram(g1, y, True)

        ready, g2 = due(DIRECT)

        @pl.when(ready & (y > 0))
        def _():
            drain(buf.at[down_band + other, g2], core_recv.at[1, g2])
            gram(g2, down, False)

        ready, g3 = due(SECOND)

        @pl.when(ready & (y == 3))
        def _():
            drain(buf.at[up_band + other, g3], core_recv.at[2, g3])
            gram(g3, up, False)

        ready, g4 = due(due_far)

        @pl.when(ready & (y >= 2))
        def _():
            drain(buf.at[far_band + other, g4], core_recv.at[3, g4])
            gram(g4, far, False)

        begin, end = s + div(s - 1, 4), s + div(s, 4) + 1
        lax.fori_loop(begin, end, front, 0)

        @pl.when((s < STEPS) & (mod(y, 2) == 0))
        def _():
            flight = FLIGHT - core

            @pl.when((s >= flight) & (s <= FEW))
            def _():
                drain(chunk(band, s - flight), own_send.at[s - flight])

            @pl.when(s >= FEW)
            def _():
                drain(chunk(band, s - flight + 1), own_send.at[s - flight + 1])

            @pl.when(y == 2)
            def _():
                send(band, s, up_band, own_send.at[s], left_recv.at[s])

            @pl.when(y == 0)
            def _():
                send(band, s, down_band, own_send.at[s], right_recv.at[s])

        @pl.when(s == 0)
        def _():
            scatter_all(NEAR // 2, NEAR)

        @pl.when(s < SPANS - 1)
        def _():
            turn(s + 1)
            scatter_all(NEAR + 2 * s, NEAR + 2 * s + 2)

        @pl.when(s == SPANS - 2)
        def _():
            scatter_all(NEAR + 2 * SPANS - 2, AHEAD + 3)

        @pl.when(y < 3)
        def _():
            lax.fori_loop(begin - LAG, end - LAG, pass_on, 0)

        j = s - LAG

        @pl.when((j >= 0) & (j < STEPS) & (y == 3))
        def _():
            drain(chunk(up_band, j), right_recv.at[j])

            @pl.when(j < BY_ONE)
            def _():
                send(up_band, j, down_band, y_send.at[2], relay_recv.at[j])

            send(up_band, j, partner, core_send.at[2], core_recv.at[2, place(j)[0]])
            drain(chunk(down_band, j), left_recv.at[j])
            send(down_band, j, partner, core_send.at[1], core_recv.at[1, place(j)[0]])

        @pl.when(y >= 2)
        def _():
            lax.fori_loop(begin - relay, end - relay, take_far, 0)

        for q in range(1, YS):

            @pl.when((s < EARLY) & (y < q))
            def _():
                out_ref[s, :, :, q * WIDE : (q + 1) * WIDE] = jnp.zeros((2, ROWS, WIDE), out_ref.dtype)

        return carry

    lax.fori_loop(0, STEPS + LAG + 1, step, 0)

    other = 1 - 2 * core
    late = GROUPS - 1

    @pl.when(core == 1)
    def _():
        drain(buf.at[partner, late], core_recv.at[0, late])

    for kind, of_band, wanted in ((1, down_band, y > 0), (2, up_band, y == 3), (3, far_band, y >= 2)):

        @pl.when(wanted)
        def _():
            drain(buf.at[of_band + other, late], core_recv.at[kind, late])

    whole = buf.at[band]
    drain(buf.at[band, :, pl.ds(0, CHANS - 1)], a2a_send)

    @pl.when(core == 0)
    def _():
        drain(whole, core_send.at[0])

    @pl.when(y < 2)
    def _():
        drain(whole, y_send.at[0])

    @pl.when(y == 1)
    def _():
        drain(xs.at[pl.ds(0, STEPS - BY_ONE)], y_send.at[2])
        drain(xs.at[pl.ds(0, STEPS // 2)], y_send.at[1])

    @pl.when(mod(y, 2) == 0)
    def _():
        @pl.when(core == 0)
        def _():
            drain(chunk(band, STEPS - 3), own_send.at[STEPS - 3])

        for last in range(STEPS - 2, STEPS):
            drain(chunk(band, last), own_send.at[last])

        for last in (STEPS - 5, STEPS - 3, STEPS - 1):
            drain(chunk(band, 0), relay_send.at[last - div(y, 2)])

    @pl.when(y > 0)
    def _():
        drain(whole, core_send.at[1])

    @pl.when(y == 3)
    def _():
        drain(xs.at[pl.ds(0, BY_ONE)], y_send.at[2])
        drain(whole, core_send.at[2])

    @pl.when(y >= 2)
    def _():
        drain(whole, core_send.at[3])


def correlate(counts, exponents, spectra):
    dma = pltpu.SemaphoreType.DMA
    outs = (
        ((EARLY, 2, ROWS, BANDS * ROWS), jnp.bfloat16),
        ((BANDS, GROUPS, CHANS, GROUP, UNIT, ROWS), jnp.bfloat16),
        ((2, GROUP, 2 * ROWS, DEPTH), jnp.bfloat16),
        ((GROUP, 8, WIDE), jnp.float32),
    )
    return pl.pallas_call(
        kernel,
        out_shape=[pltpu.VMEM(*out) for out in outs],
        in_specs=[pl.BlockSpec(memory_space=pltpu.HBM)] * 3,
        out_specs=[pl.BlockSpec(memory_space=pltpu.VMEM)] * 4,
        scratch_shapes=[
            pltpu.SMEM((OWN,), jnp.int32),
            pltpu.VMEM((CHANS, UNIT, ROWS), jnp.int32),
            pltpu.VMEM((ROWS, CHANS * OWN), jnp.int32),
            pltpu.VMEM((SPANS, 2, ROWS * SAMPLES, LANES), jnp.bfloat16),
            pltpu.VMEM((2, ROWS * SAMPLES, LANES), jnp.float32),
            pltpu.VMEM((LANES * UNIT, ROWS), jnp.float32),
            pltpu.VMEM((CHANS, GROUPS, GROUP, UNIT, ROWS), jnp.bfloat16),
            dma((SPANS + 2,)),
            dma((STEPS,)), dma((STEPS,)), dma((STEPS,)), dma((STEPS,)), dma((4, GROUPS)),
            dma, dma((3,)), dma((STEPS,)), dma((STEPS,)), dma((4,)),
        ],
        compiler_params=pltpu.CompilerParams(
            collective_id=0, has_side_effects=True, vmem_limit_bytes=12 << 20
        ),
        name="correlate",
    )(*(pltpu.with_memory_space_constraint(operand, pltpu.HBM) for operand in (counts, exponents, spectra)))


def finish_kernel(early_ref, buf, forms, shares, out_ref, stage, early_sem, late_sem):
    band = lax.axis_index("band")
    copies = []
    for n in range(OUT_PARTS):
        part = pl.ds(n * (EARLY // OUT_PARTS), EARLY // OUT_PARTS)
        copies.append(pltpu.make_async_copy(early_ref.at[part], out_ref.at[part], early_sem.at[n]))
    for copy in copies:
        copy.start()
    late = GROUPS - 1
    for c in range(GROUP):
        for q in range(YS):
            columns = pl.ds(q * WIDE, WIDE)
            right = jnp.concatenate(
                [buf[2 * q, late, :, c].reshape(DEPTH, ROWS), buf[2 * q + 1, late, :, c].reshape(DEPTH, ROWS)], axis=1
            )
            product = jnp.dot(forms[late % 2, c], right, preferred_element_type=jnp.float32) * shares[c, :1]
            for part in range(2):
                tile = lower(product[part * ROWS : (part + 1) * ROWS], band * ROWS - q * WIDE)
                stage[c, part, :, columns] = tile.astype(jnp.bfloat16)

        copies.append(pltpu.make_async_copy(stage.at[c], out_ref.at[EARLY + c], late_sem.at[c]))
        copies[-1].start()
    for copy in copies:
        copy.wait()


def finish(early, buf, forms, shares):
    vmem = pl.BlockSpec(memory_space=pltpu.VMEM)
    return pl.pallas_call(
        finish_kernel,
        out_shape=jax.ShapeDtypeStruct((OWN, 2, ROWS, BANDS * ROWS), jnp.bfloat16),
        in_specs=[vmem] * 4,
        out_specs=pl.BlockSpec(memory_space=pl.ANY),
        scratch_shapes=[
            pltpu.VMEM((GROUP, 2, ROWS, BANDS * ROWS), jnp.bfloat16),
            pltpu.SemaphoreType.DMA((OUT_PARTS,)),
            pltpu.SemaphoreType.DMA((GROUP,)),
        ],
        compiler_params=pltpu.CompilerParams(vmem_limit_bytes=12 << 20),
        name="finish",
    )(*(pltpu.with_memory_space_constraint(operand, pltpu.VMEM) for operand in (early, buf, forms, shares)))


def local(spectra, exponents, counts):
    flat = jnp.transpose(spectra, (0, 1, 3, 2)).reshape(2, ROWS * SAMPLES, CHANS * OWN)
    return finish(*correlate(counts, exponents, flat))


def solution(mesh):
    placed = (P(None, "band", None, "chan"), P("band", None), P("chan"))
    return jax.shard_map(
        local, mesh=mesh, in_specs=placed, out_specs=P("chan", None, "band", None), check_vma=False
    )
```

```python
import jax
import jax.numpy as jnp
from jax import lax
from jax.experimental import pallas as pl
from jax.experimental.pallas import tpu as pltpu
from jax.sharding import PartitionSpec as P

MESH = pl.DeviceIdType.MESH
BLOCK = 64
BANDS, CORES, YS = 8, 2, 4
ZS, XS = 8, 4
CHANS = ZS * XS
ROWS = 128
OWN = 16
SAMPLES = 8
UNIT = 2 * SAMPLES
DEPTH = CHANS * UNIT
WIDE = 2 * ROWS
GROUPS = 4
GROUP = OWN // GROUPS
EARLY = OWN - GROUP
CHUNK = 4
PARTS = CHANS // CHUNK
STEPS = GROUPS * PARTS
WHOLE = 12, 17, 22, 27
DIRECT = 17, 23, 29
SECOND = 19, 25, 31
AHEAD = 16
BY_ONE = 24
LANES = 128
SPANS = CHANS * OWN // LANES
LAG = 3
NEAR = 2 * GROUPS
FEW = 28
FLIGHT = 4
OUT_PARTS = 6


def power_scale(exponents):
    scale = jnp.zeros(exponents.shape, jnp.float32)
    for power in range(-2, 3):
        scale = scale + jnp.where(exponents == power, jnp.float32(2.0**power), jnp.float32(0.0))
    return scale


def mod(a, n):
    return a % n if isinstance(a, int) else lax.rem(a, jnp.full_like(a, n))


def div(a, n):
    return a // n if isinstance(a, int) else lax.div(a, jnp.full_like(a, n))


def flip(a, b, bits):
    return sum(mod(div(a, 1 << n) + div(b, 1 << n), 2) * (1 << n) for n in range(bits))


def offset(k):
    return 2 * div(k, 2 * CHUNK) + mod(k, 2), div(mod(k, CHUNK), 2) + 2 * mod(div(k, CHUNK), 2)


def place(s):
    near = int(s < NEAR) if isinstance(s, int) else (s < NEAR).astype(jnp.int32)
    rest = s - NEAR
    group = near * div(s, 2) + (1 - near) * div(rest, PARTS - 2)
    return group, near * mod(s, 2) + (1 - near) * (2 + mod(rest, PARTS - 2))


def source(chan, k):
    dz, dx = offset(k)
    return flip(div(chan, XS), dz, 3) * XS + mod(mod(chan, XS) + dx, XS)


def target(chan, k):
    dz, dx = offset(k)
    return flip(div(chan, XS), dz, 3) * XS + mod(mod(chan, XS) + XS - dx, XS)


def lower(tile, first):
    line = lax.broadcasted_iota(jnp.int32, tile.shape, 0)
    column = lax.broadcasted_iota(jnp.int32, tile.shape, 1)
    limit = jnp.where(line < BLOCK, BLOCK, 2 * BLOCK) + first
    return jnp.where(column < limit, tile, 0.0)


def kernel(
    counts_hbm, exponents_ref, x_ref, out_ref, buf, forms, shares, counts_ref, times, powers, raw, wide, narrow, xs, load_sem,
    a2a_recv, left_recv, right_recv, relay_recv, core_recv, a2a_send, y_send, own_send, relay_send, core_send,
):
    band = lax.axis_index("band")
    chan = lax.axis_index("chan")
    y, core = div(band, CORES), mod(band, CORES)
    partner = band + 1 - 2 * core
    up, down, far = mod(y + 1, YS), mod(y + YS - 1, YS), mod(y + 2, YS)
    slow = (y == 2).astype(jnp.int32)
    relay = 9 + 3 * slow
    due_far = 20 + slow, 24 + 2 * slow, 30 + slow
    up_band, down_band, far_band = up * CORES + core, down * CORES + core, far * CORES + core

    barrier = pltpu.get_barrier_semaphore()

    def greet(k, carry):
        pl.semaphore_signal(barrier, inc=1, device_id=(band, target(chan, k)), device_id_type=MESH)
        return carry

    def drain(ref, sem):
        pltpu.make_async_copy(ref, ref, sem).wait()

    def span(n):
        return flip(div(chan, 2 * XS), n, 2)

    def lanes(n):
        return pl.ds(pl.multiple_of(span(n) * LANES, LANES), LANES)

    loads = [
        pltpu.make_async_copy(exponents_ref, powers, load_sem.at[SPANS]),
        pltpu.make_async_copy(counts_hbm, counts_ref, load_sem.at[SPANS + 1]),
    ] + [pltpu.make_async_copy(x_ref.at[:, :, lanes(n)], raw.at[n], load_sem.at[n]) for n in range(SPANS)]
    for load in loads:
        load.start()

    for other in (up_band, down_band, partner):
        pl.semaphore_signal(barrier, inc=1, device_id=(other, chan), device_id_type=MESH)
    lax.fori_loop(1, CHANS, greet, 0)

    def turn(n):
        drain(raw.at[n], load_sem.at[n])
        scale = power_scale(powers[:, lanes(n)])
        for part in range(2):
            wide[part] = raw[n, part].astype(jnp.float32)
            for t in range(SAMPLES):
                tile = wide[part, pl.ds(t, ROWS, stride=SAMPLES), :] * scale
                narrow[pl.ds(part * SAMPLES + t, LANES, stride=UNIT), :] = tile.T

        def pack(d, carry):
            own = narrow[pl.ds(pl.multiple_of(d * (OWN * UNIT), OWN * UNIT), OWN * UNIT), :]
            xs[span(n) * (LANES // OWN) + d] = own.astype(jnp.bfloat16).reshape(GROUPS, GROUP, UNIT, ROWS)
            return carry

        lax.fori_loop(0, LANES // OWN, pack, 0)

    loads[0].wait()
    turn(0)
    for g in range(GROUPS):
        pltpu.make_async_copy(xs.at[chan, g], buf.at[band, g, 0], a2a_recv.at[2 * g]).start()

    pl.semaphore_wait(barrier, CHANS + 2)

    def scatter(s):
        g, part = place(s)

        for n in range(CHUNK):
            k = part * CHUNK + n
            to = target(chan, k)

            @pl.when(k > 0)
            def _():
                pltpu.make_async_remote_copy(
                    src_ref=xs.at[to, g], dst_ref=buf.at[band, g, k],
                    send_sem=a2a_send, recv_sem=a2a_recv.at[s],
                    device_id=(band, to), device_id_type=MESH,
                ).start()

    def scatter_all(first, end):
        def one(s, carry):
            scatter(s)
            return carry

        lax.fori_loop(first, end, one, 0)

    scatter_all(0, NEAR // 2)

    piece = lax.broadcasted_iota(jnp.int32, times.shape, 0)
    row = lax.broadcasted_iota(jnp.int32, times.shape, 1)
    times[...] = source(chan, piece) * SAMPLES + mod(row, SAMPLES)
    loads[1].wait()
    for c in range(GROUP):
        shares[c] = 1.0 / jnp.full(shares.shape[1:], counts_ref[EARLY + c], jnp.int32).astype(jnp.float32)

    def chunk(of_band, s):
        g, part = place(s)
        return buf.at[of_band, g, pl.ds(part * CHUNK, CHUNK)]

    def send(of_band, s, to_band, send_sem, recv_sem):
        ref = chunk(of_band, s)
        pltpu.make_async_remote_copy(
            src_ref=ref, dst_ref=ref, send_sem=send_sem, recv_sem=recv_sem,
            device_id=(to_band, chan), device_id_type=MESH,
        ).start()

    def prepare(g, c):
        slot = mod(g, 2)
        own = buf[band, g, :, c].astype(jnp.float32)
        own = jnp.where(times[...] < counts_ref[g * GROUP + c], own, 0.0)
        swapped = jnp.concatenate([own[:, SAMPLES:], -own[:, :SAMPLES]], axis=1)
        forms[slot, c, :ROWS] = own.astype(jnp.bfloat16).reshape(DEPTH, ROWS).T
        forms[slot, c, ROWS:] = swapped.astype(jnp.bfloat16).reshape(DEPTH, ROWS).T

    def gram(g, q, diagonal):
        slot = mod(g, 2)
        columns = pl.ds(pl.multiple_of(q * WIDE, WIDE), WIDE)

        for c in range(GROUP):
            right = jnp.concatenate(
                [buf[2 * q, g, :, c].reshape(DEPTH, ROWS), buf[2 * q + 1, g, :, c].reshape(DEPTH, ROWS)], axis=1
            )
            share = 1.0 / jnp.full((1, WIDE), counts_ref[g * GROUP + c], jnp.int32).astype(jnp.float32)
            product = jnp.dot(forms[slot, c], right, preferred_element_type=jnp.float32) * share
            for part in range(2):
                tile = product[part * ROWS : (part + 1) * ROWS]
                if diagonal:
                    tile = lower(tile, core * ROWS)
                out_ref[g * GROUP + c, part, :, columns] = tile.astype(jnp.bfloat16)

    def front(s, carry):
        @pl.when(s < STEPS)
        def _():
            drain(chunk(band, s), a2a_recv.at[s])

            @pl.when(y < 2)
            def _():
                send(band, s, up_band, y_send.at[0], left_recv.at[s])

            @pl.when((y == 1) & (mod(s, 2) == 1))
            def _():
                send(band, s, down_band, y_send.at[1], right_recv.at[s])

            @pl.when((core == 0) & ((mod(y, 2) == 1) | (place(s)[0] < GROUPS - 1)))
            def _():
                send(band, s, partner, core_send.at[0], core_recv.at[0, place(s)[0]])

        @pl.when((s > 2) & (s + AHEAD < STEPS))
        def _():
            scatter(s + AHEAD)

        return carry

    def pass_on(j, carry):
        @pl.when((j >= 0) & (j < STEPS) & (y == 0) & (mod(j, 2) == 1))
        def _():
            drain(chunk(up_band, j), right_recv.at[j])

            @pl.when(j >= 7)
            def _():
                drain(chunk(up_band, j - 6), relay_send.at[j - 6])

            send(up_band, j, down_band, relay_send.at[j], relay_recv.at[j])

        @pl.when((j >= 0) & (j < STEPS) & (y > 0))
        def _():
            drain(chunk(down_band, j), left_recv.at[j])

            @pl.when((y == 1) & (j >= BY_ONE))
            def _():
                send(down_band, j, up_band, y_send.at[2], relay_recv.at[j])

            @pl.when((y == 2) & (mod(j, 2) == 0))
            def _():
                @pl.when(j >= 6)
                def _():
                    drain(chunk(down_band, j - 6), relay_send.at[j - 6])

                send(down_band, j, up_band, relay_send.at[j], relay_recv.at[j])

            send(down_band, j, partner, core_send.at[1], core_recv.at[1, place(j)[0]])

        return carry

    def take_far(i, carry):
        @pl.when((i >= 0) & (i < STEPS))
        def _():
            drain(chunk(far_band, i), relay_recv.at[i])

            @pl.when((y == 3) | (place(i)[0] < GROUPS - 1))
            def _():
                send(far_band, i, partner, core_send.at[3], core_recv.at[3, place(i)[0]])

        return carry

    def step(s, carry):
        def due(steps):
            ready = (s == steps[0]) | (s == steps[1]) | (s == steps[2])
            return ready, (s >= steps[1]).astype(jnp.int32) + (s >= steps[2]).astype(jnp.int32)

        other = 1 - 2 * core

        begun = [s >= first for first in WHOLE]
        g1 = sum(one.astype(jnp.int32) for one in begun) - 1
        since = s - WHOLE[0]
        for one, first, last in zip(begun[1:], WHOLE[1:], WHOLE[:-1]):
            since = since - one.astype(jnp.int32) * (first - last)

        @pl.when((since >= 0) & (since < GROUP))
        def _():
            prepare(g1, since)

        @pl.when((since == GROUP) & (g1 < GROUPS - 1))
        def _():
            @pl.when(core == 1)
            def _():
                drain(buf.at[partner, g1], core_recv.at[0, g1])

            gram(g1, y, True)

        ready, g2 = due(DIRECT)

        @pl.when(ready & (y > 0))
        def _():
            drain(buf.at[down_band + other, g2], core_recv.at[1, g2])
            gram(g2, down, False)

        ready, g3 = due(SECOND)

        @pl.when(ready & (y == 3))
        def _():
            drain(buf.at[up_band + other, g3], core_recv.at[2, g3])
            gram(g3, up, False)

        ready, g4 = due(due_far)

        @pl.when(ready & (y >= 2))
        def _():
            drain(buf.at[far_band + other, g4], core_recv.at[3, g4])
            gram(g4, far, False)

        begin, end = s + div(s - 1, 4), s + div(s, 4) + 1
        lax.fori_loop(begin, end, front, 0)

        @pl.when((s < STEPS) & (mod(y, 2) == 0))
        def _():
            flight = FLIGHT - core

            @pl.when((s >= flight) & (s <= FEW))
            def _():
                drain(chunk(band, s - flight), own_send.at[s - flight])

            @pl.when(s >= FEW)
            def _():
                drain(chunk(band, s - flight + 1), own_send.at[s - flight + 1])

            @pl.when(y == 2)
            def _():
                send(band, s, up_band, own_send.at[s], left_recv.at[s])

            @pl.when(y == 0)
            def _():
                send(band, s, down_band, own_send.at[s], right_recv.at[s])

        @pl.when(s == 0)
        def _():
            scatter_all(NEAR // 2, NEAR)

        @pl.when(s < SPANS - 1)
        def _():
            turn(s + 1)
            scatter_all(NEAR + 2 * s, NEAR + 2 * s + 2)

        @pl.when(s == SPANS - 2)
        def _():
            scatter_all(NEAR + 2 * SPANS - 2, AHEAD + 3)

        @pl.when(y < 3)
        def _():
            lax.fori_loop(begin - LAG, end - LAG, pass_on, 0)

        j = s - LAG

        @pl.when((j >= 0) & (j < STEPS) & (y == 3))
        def _():
            drain(chunk(up_band, j), right_recv.at[j])

            @pl.when(j < BY_ONE)
            def _():
                send(up_band, j, down_band, y_send.at[2], relay_recv.at[j])

            send(up_band, j, partner, core_send.at[2], core_recv.at[2, place(j)[0]])
            drain(chunk(down_band, j), left_recv.at[j])
            send(down_band, j, partner, core_send.at[1], core_recv.at[1, place(j)[0]])

        @pl.when(y >= 2)
        def _():
            lax.fori_loop(begin - relay, end - relay, take_far, 0)

        for q in range(1, YS):

            @pl.when((s < EARLY) & (y < q))
            def _():
                out_ref[s, :, :, q * WIDE : (q + 1) * WIDE] = jnp.zeros((2, ROWS, WIDE), out_ref.dtype)

        return carry

    lax.fori_loop(0, STEPS + LAG + 1, step, 0)

    other = 1 - 2 * core
    late = GROUPS - 1

    @pl.when(mod(y, 2) == 0)
    def _():
        @pl.when(core == 0)
        def _():
            drain(chunk(band, STEPS - 3), own_send.at[STEPS - 3])

        for last in range(STEPS - 2, STEPS):
            drain(chunk(band, last), own_send.at[last])

        for last in (STEPS - 5, STEPS - 3, STEPS - 1):
            drain(chunk(band, 0), relay_send.at[last - div(y, 2)])

    def send_late(of_band, send_sem, recv_sem):
        ref = buf.at[of_band, late]
        pltpu.make_async_remote_copy(
            src_ref=ref, dst_ref=ref, send_sem=send_sem, recv_sem=recv_sem,
            device_id=(partner, chan), device_id_type=MESH,
        ).start()

    @pl.when((core == 0) & (mod(y, 2) == 0))
    def _():
        send_late(band, core_send.at[0], core_recv.at[0, late])

    @pl.when(y == 2)
    def _():
        send_late(far_band, core_send.at[3], core_recv.at[3, late])

    @pl.when(core == 1)
    def _():
        drain(buf.at[partner, late], core_recv.at[0, late])

    for kind, of_band, wanted in ((1, down_band, y > 0), (2, up_band, y == 3), (3, far_band, y >= 2)):

        @pl.when(wanted)
        def _():
            drain(buf.at[of_band + other, late], core_recv.at[kind, late])

    whole = buf.at[band]
    drain(buf.at[band, :, pl.ds(0, CHANS - 1)], a2a_send)

    @pl.when(core == 0)
    def _():
        drain(whole, core_send.at[0])

    @pl.when(y < 2)
    def _():
        drain(whole, y_send.at[0])

    @pl.when(y == 1)
    def _():
        drain(xs.at[pl.ds(0, STEPS - BY_ONE)], y_send.at[2])
        drain(xs.at[pl.ds(0, STEPS // 2)], y_send.at[1])

    @pl.when(y > 0)
    def _():
        drain(whole, core_send.at[1])

    @pl.when(y == 3)
    def _():
        drain(xs.at[pl.ds(0, BY_ONE)], y_send.at[2])
        drain(whole, core_send.at[2])

    @pl.when(y >= 2)
    def _():
        drain(whole, core_send.at[3])


def correlate(counts, exponents, spectra):
    dma = pltpu.SemaphoreType.DMA
    outs = (
        ((EARLY, 2, ROWS, BANDS * ROWS), jnp.bfloat16),
        ((BANDS, GROUPS, CHANS, GROUP, UNIT, ROWS), jnp.bfloat16),
        ((2, GROUP, 2 * ROWS, DEPTH), jnp.bfloat16),
        ((GROUP, 8, WIDE), jnp.float32),
    )
    return pl.pallas_call(
        kernel,
        out_shape=[pltpu.VMEM(*out) for out in outs],
        in_specs=[pl.BlockSpec(memory_space=pltpu.HBM)] * 3,
        out_specs=[pl.BlockSpec(memory_space=pltpu.VMEM)] * 4,
        scratch_shapes=[
            pltpu.SMEM((OWN,), jnp.int32),
            pltpu.VMEM((CHANS, UNIT, ROWS), jnp.int32),
            pltpu.VMEM((ROWS, CHANS * OWN), jnp.int32),
            pltpu.VMEM((SPANS, 2, ROWS * SAMPLES, LANES), jnp.bfloat16),
            pltpu.VMEM((2, ROWS * SAMPLES, LANES), jnp.float32),
            pltpu.VMEM((LANES * UNIT, ROWS), jnp.float32),
            pltpu.VMEM((CHANS, GROUPS, GROUP, UNIT, ROWS), jnp.bfloat16),
            dma((SPANS + 2,)),
            dma((STEPS,)), dma((STEPS,)), dma((STEPS,)), dma((STEPS,)), dma((4, GROUPS)),
            dma, dma((3,)), dma((STEPS,)), dma((STEPS,)), dma((4,)),
        ],
        compiler_params=pltpu.CompilerParams(
            collective_id=0, has_side_effects=True, vmem_limit_bytes=12 << 20
        ),
        name="correlate",
    )(*(pltpu.with_memory_space_constraint(operand, pltpu.HBM) for operand in (counts, exponents, spectra)))


def finish_kernel(early_ref, buf, forms, shares, out_ref, stage, early_sem, late_sem):
    band = lax.axis_index("band")
    copies = []
    for n in range(OUT_PARTS):
        part = pl.ds(n * (EARLY // OUT_PARTS), EARLY // OUT_PARTS)
        copies.append(pltpu.make_async_copy(early_ref.at[part], out_ref.at[part], early_sem.at[n]))
    for copy in copies:
        copy.start()
    late = GROUPS - 1
    for c in range(GROUP):
        for q in range(YS):
            columns = pl.ds(q * WIDE, WIDE)
            right = jnp.concatenate(
                [buf[2 * q, late, :, c].reshape(DEPTH, ROWS), buf[2 * q + 1, late, :, c].reshape(DEPTH, ROWS)], axis=1
            )
            product = jnp.dot(forms[late % 2, c], right, preferred_element_type=jnp.float32) * shares[c, :1]
            for part in range(2):
                tile = lower(product[part * ROWS : (part + 1) * ROWS], band * ROWS - q * WIDE)
                stage[c, part, :, columns] = tile.astype(jnp.bfloat16)

        copies.append(pltpu.make_async_copy(stage.at[c], out_ref.at[EARLY + c], late_sem.at[c]))
        copies[-1].start()
    for copy in copies:
        copy.wait()


def finish(early, buf, forms, shares):
    vmem = pl.BlockSpec(memory_space=pltpu.VMEM)
    return pl.pallas_call(
        finish_kernel,
        out_shape=jax.ShapeDtypeStruct((OWN, 2, ROWS, BANDS * ROWS), jnp.bfloat16),
        in_specs=[vmem] * 4,
        out_specs=pl.BlockSpec(memory_space=pl.ANY),
        scratch_shapes=[
            pltpu.VMEM((GROUP, 2, ROWS, BANDS * ROWS), jnp.bfloat16),
            pltpu.SemaphoreType.DMA((OUT_PARTS,)),
            pltpu.SemaphoreType.DMA((GROUP,)),
        ],
        compiler_params=pltpu.CompilerParams(vmem_limit_bytes=12 << 20),
        name="finish",
    )(*(pltpu.with_memory_space_constraint(operand, pltpu.VMEM) for operand in (early, buf, forms, shares)))


def local(spectra, exponents, counts):
    flat = jnp.transpose(spectra, (0, 1, 3, 2)).reshape(2, ROWS * SAMPLES, CHANS * OWN)
    return finish(*correlate(counts, exponents, flat))


def solution(mesh):
    placed = (P(None, "band", None, "chan"), P("band", None), P("chan"))
    return jax.shard_map(
        local, mesh=mesh, in_specs=placed, out_specs=P("chan", None, "band", None), check_vma=False
    )
```

```python
import jax
import jax.numpy as jnp
from jax import lax
from jax.experimental import pallas as pl
from jax.experimental.pallas import tpu as pltpu
from jax.sharding import PartitionSpec as P

MESH = pl.DeviceIdType.MESH
BLOCK = 64
BANDS, CORES, YS = 8, 2, 4
ZS, XS = 8, 4
CHANS = ZS * XS
ROWS = 128
OWN = 16
SAMPLES = 8
UNIT = 2 * SAMPLES
DEPTH = CHANS * UNIT
WIDE = 2 * ROWS
GROUPS = 4
GROUP = OWN // GROUPS
EARLY = OWN - GROUP
CHUNK = 4
PARTS = CHANS // CHUNK
STEPS = GROUPS * PARTS
WHOLE = 12, 17, 22, 26
DIRECT = 17, 23, 29
SECOND = 19, 25, 31
AHEAD = 16
BY_ONE = 24
LANES = 128
SPANS = CHANS * OWN // LANES
LAG = 3
NEAR = 2 * GROUPS
FEW = 28
FLIGHT = 4
OUT_PARTS = 6


def power_scale(exponents):
    scale = jnp.zeros(exponents.shape, jnp.float32)
    for power in range(-2, 3):
        scale = scale + jnp.where(exponents == power, jnp.float32(2.0**power), jnp.float32(0.0))
    return scale


def mod(a, n):
    return a % n if isinstance(a, int) else lax.rem(a, jnp.full_like(a, n))


def div(a, n):
    return a // n if isinstance(a, int) else lax.div(a, jnp.full_like(a, n))


def flip(a, b, bits):
    return sum(mod(div(a, 1 << n) + div(b, 1 << n), 2) * (1 << n) for n in range(bits))


def offset(k):
    return 2 * div(k, 2 * CHUNK) + mod(k, 2), div(mod(k, CHUNK), 2) + 2 * mod(div(k, CHUNK), 2)


def place(s):
    near = int(s < NEAR) if isinstance(s, int) else (s < NEAR).astype(jnp.int32)
    rest = s - NEAR
    group = near * div(s, 2) + (1 - near) * div(rest, PARTS - 2)
    return group, near * mod(s, 2) + (1 - near) * (2 + mod(rest, PARTS - 2))


def source(chan, k):
    dz, dx = offset(k)
    return flip(div(chan, XS), dz, 3) * XS + mod(mod(chan, XS) + dx, XS)


def target(chan, k):
    dz, dx = offset(k)
    return flip(div(chan, XS), dz, 3) * XS + mod(mod(chan, XS) + XS - dx, XS)


def lower(tile, first):
    line = lax.broadcasted_iota(jnp.int32, tile.shape, 0)
    column = lax.broadcasted_iota(jnp.int32, tile.shape, 1)
    limit = jnp.where(line < BLOCK, BLOCK, 2 * BLOCK) + first
    return jnp.where(column < limit, tile, 0.0)


def kernel(
    counts_hbm, exponents_ref, x_ref, out_ref, buf, forms, shares, counts_ref, times, powers, raw, wide, narrow, xs, load_sem,
    a2a_recv, left_recv, right_recv, relay_recv, core_recv, a2a_send, y_send, own_send, relay_send, core_send,
):
    band = lax.axis_index("band")
    chan = lax.axis_index("chan")
    y, core = div(band, CORES), mod(band, CORES)
    partner = band + 1 - 2 * core
    up, down, far = mod(y + 1, YS), mod(y + YS - 1, YS), mod(y + 2, YS)
    slow = (y == 2).astype(jnp.int32)
    relay = 9 + 3 * slow
    due_far = 20 + slow, 24 + 2 * slow, 30 + slow
    up_band, down_band, far_band = up * CORES + core, down * CORES + core, far * CORES + core

    barrier = pltpu.get_barrier_semaphore()

    def greet(k, carry):
        pl.semaphore_signal(barrier, inc=1, device_id=(band, target(chan, k)), device_id_type=MESH)
        return carry

    def drain(ref, sem):
        pltpu.make_async_copy(ref, ref, sem).wait()

    def span(n):
        return flip(div(chan, 2 * XS), n, 2)

    def lanes(n):
        return pl.ds(pl.multiple_of(span(n) * LANES, LANES), LANES)

    loads = [
        pltpu.make_async_copy(exponents_ref, powers, load_sem.at[SPANS]),
        pltpu.make_async_copy(counts_hbm, counts_ref, load_sem.at[SPANS + 1]),
    ] + [pltpu.make_async_copy(x_ref.at[:, :, lanes(n)], raw.at[n], load_sem.at[n]) for n in range(SPANS)]
    for load in loads:
        load.start()

    for other in (up_band, down_band, partner):
        pl.semaphore_signal(barrier, inc=1, device_id=(other, chan), device_id_type=MESH)
    lax.fori_loop(1, CHANS, greet, 0)

    def turn(n):
        drain(raw.at[n], load_sem.at[n])
        scale = power_scale(powers[:, lanes(n)])
        for part in range(2):
            wide[part] = raw[n, part].astype(jnp.float32)
            for t in range(SAMPLES):
                tile = wide[part, pl.ds(t, ROWS, stride=SAMPLES), :] * scale
                narrow[pl.ds(part * SAMPLES + t, LANES, stride=UNIT), :] = tile.astype(jnp.bfloat16).T.astype(jnp.float32)

        def pack(d, carry):
            own = narrow[pl.ds(pl.multiple_of(d * (OWN * UNIT), OWN * UNIT), OWN * UNIT), :]
            xs[span(n) * (LANES // OWN) + d] = own.astype(jnp.bfloat16).reshape(GROUPS, GROUP, UNIT, ROWS)
            return carry

        lax.fori_loop(0, LANES // OWN, pack, 0)

    loads[0].wait()
    turn(0)
    for g in range(GROUPS):
        pltpu.make_async_copy(xs.at[chan, g], buf.at[band, g, 0], a2a_recv.at[2 * g]).start()

    pl.semaphore_wait(barrier, CHANS + 2)

    def scatter(s):
        g, part = place(s)

        for n in range(CHUNK):
            k = part * CHUNK + n
            to = target(chan, k)

            @pl.when(k > 0)
            def _():
                pltpu.make_async_remote_copy(
                    src_ref=xs.at[to, g], dst_ref=buf.at[band, g, k],
                    send_sem=a2a_send, recv_sem=a2a_recv.at[s],
                    device_id=(band, to), device_id_type=MESH,
                ).start()

    def scatter_all(first, end):
        def one(s, carry):
            scatter(s)
            return carry

        lax.fori_loop(first, end, one, 0)

    scatter_all(0, NEAR // 2)

    piece = lax.broadcasted_iota(jnp.int32, times.shape, 0)
    row = lax.broadcasted_iota(jnp.int32, times.shape, 1)
    times[...] = source(chan, piece) * SAMPLES + mod(row, SAMPLES)
    loads[1].wait()
    for c in range(GROUP):
        shares[c] = 1.0 / jnp.full(shares.shape[1:], counts_ref[EARLY + c], jnp.int32).astype(jnp.float32)

    def chunk(of_band, s):
        g, part = place(s)
        return buf.at[of_band, g, pl.ds(part * CHUNK, CHUNK)]

    def send(of_band, s, to_band, send_sem, recv_sem):
        ref = chunk(of_band, s)
        pltpu.make_async_remote_copy(
            src_ref=ref, dst_ref=ref, send_sem=send_sem, recv_sem=recv_sem,
            device_id=(to_band, chan), device_id_type=MESH,
        ).start()

    def prepare(g, c):
        slot = mod(g, 2)
        own = buf[band, g, :, c].astype(jnp.float32)
        own = jnp.where(times[...] < counts_ref[g * GROUP + c], own, 0.0)
        swapped = jnp.concatenate([own[:, SAMPLES:], -own[:, :SAMPLES]], axis=1)
        forms[slot, c, :ROWS] = own.astype(jnp.bfloat16).reshape(DEPTH, ROWS).T
        forms[slot, c, ROWS:] = swapped.astype(jnp.bfloat16).reshape(DEPTH, ROWS).T

    def gram(g, q, diagonal):
        slot = mod(g, 2)
        columns = pl.ds(pl.multiple_of(q * WIDE, WIDE), WIDE)

        for c in range(GROUP):
            right = jnp.concatenate(
                [buf[2 * q, g, :, c].reshape(DEPTH, ROWS), buf[2 * q + 1, g, :, c].reshape(DEPTH, ROWS)], axis=1
            )
            share = 1.0 / jnp.full((1, WIDE), counts_ref[g * GROUP + c], jnp.int32).astype(jnp.float32)
            product = jnp.dot(forms[slot, c], right, preferred_element_type=jnp.float32) * share
            for part in range(2):
                tile = product[part * ROWS : (part + 1) * ROWS]
                if diagonal:
                    tile = lower(tile, core * ROWS)
                out_ref[g * GROUP + c, part, :, columns] = tile.astype(jnp.bfloat16)

    def front(s, carry):
        @pl.when(s < STEPS)
        def _():
            drain(chunk(band, s), a2a_recv.at[s])

            @pl.when(y < 2)
            def _():
                send(band, s, up_band, y_send.at[0], left_recv.at[s])

            @pl.when((y == 1) & (mod(s, 2) == 1))
            def _():
                send(band, s, down_band, y_send.at[1], right_recv.at[s])

            @pl.when(core == 0)
            def _():
                send(band, s, partner, core_send.at[0], core_recv.at[0, place(s)[0]])

        @pl.when((s > 2) & (s + AHEAD < STEPS))
        def _():
            scatter(s + AHEAD)

        return carry

    def pass_on(j, carry):
        @pl.when((j >= 0) & (j < STEPS) & (y == 0) & (mod(j, 2) == 1))
        def _():
            drain(chunk(up_band, j), right_recv.at[j])

            @pl.when(j >= 7)
            def _():
                drain(chunk(up_band, j - 6), relay_send.at[j - 6])

            send(up_band, j, down_band, relay_send.at[j], relay_recv.at[j])

        @pl.when((j >= 0) & (j < STEPS) & (y > 0))
        def _():
            drain(chunk(down_band, j), left_recv.at[j])

            @pl.when((y == 1) & (j >= BY_ONE))
            def _():
                send(down_band, j, up_band, y_send.at[2], relay_recv.at[j])

            @pl.when((y == 2) & (mod(j, 2) == 0))
            def _():
                @pl.when(j >= 6)
                def _():
                    drain(chunk(down_band, j - 6), relay_send.at[j - 6])

                send(down_band, j, up_band, relay_send.at[j], relay_recv.at[j])

            send(down_band, j, partner, core_send.at[1], core_recv.at[1, place(j)[0]])

        return carry

    def take_far(i, carry):
        @pl.when((i >= 0) & (i < STEPS))
        def _():
            drain(chunk(far_band, i), relay_recv.at[i])
            send(far_band, i, partner, core_send.at[3], core_recv.at[3, place(i)[0]])

        return carry

    def step(s, carry):
        def due(steps):
            ready = (s == steps[0]) | (s == steps[1]) | (s == steps[2])
            return ready, (s >= steps[1]).astype(jnp.int32) + (s >= steps[2]).astype(jnp.int32)

        other = 1 - 2 * core

        ready, g2 = due(DIRECT)

        @pl.when(ready & (y > 0))
        def _():
            drain(buf.at[down_band + other, g2], core_recv.at[1, g2])
            gram(g2, down, False)

        ready, g3 = due(SECOND)

        @pl.when(ready & (y == 3))
        def _():
            drain(buf.at[up_band + other, g3], core_recv.at[2, g3])
            gram(g3, up, False)

        ready, g4 = due(due_far)

        @pl.when(ready & (y >= 2))
        def _():
            drain(buf.at[far_band + other, g4], core_recv.at[3, g4])
            gram(g4, far, False)

        begun = [s >= first for first in WHOLE]
        g1 = sum(one.astype(jnp.int32) for one in begun) - 1
        since = s - WHOLE[0]
        for one, first, last in zip(begun[1:], WHOLE[1:], WHOLE[:-1]):
            since = since - one.astype(jnp.int32) * (first - last)

        @pl.when((since >= 0) & (since < GROUP))
        def _():
            prepare(g1, since)

        @pl.when((since == GROUP - 1) & (g1 < GROUPS - 1))
        def _():
            @pl.when(core == 1)
            def _():
                drain(buf.at[partner, g1], core_recv.at[0, g1])

            gram(g1, y, True)

        begin, end = s + div(s - 1, 4), s + div(s, 4) + 1
        lax.fori_loop(begin, end, front, 0)

        @pl.when((s < STEPS) & (mod(y, 2) == 0))
        def _():
            flight = FLIGHT - core

            @pl.when((s >= flight) & (s <= FEW))
            def _():
                drain(chunk(band, s - flight), own_send.at[s - flight])

            @pl.when(s >= FEW)
            def _():
                drain(chunk(band, s - flight + 1), own_send.at[s - flight + 1])

            @pl.when(y == 2)
            def _():
                send(band, s, up_band, own_send.at[s], left_recv.at[s])

            @pl.when(y == 0)
            def _():
                send(band, s, down_band, own_send.at[s], right_recv.at[s])

        @pl.when(s == 0)
        def _():
            scatter_all(NEAR // 2, NEAR)

        @pl.when(s < SPANS - 1)
        def _():
            turn(s + 1)
            scatter_all(NEAR + 2 * s, NEAR + 2 * s + 2)

        @pl.when(s == SPANS - 2)
        def _():
            scatter_all(NEAR + 2 * SPANS - 2, AHEAD + 3)

        @pl.when(y < 3)
        def _():
            lax.fori_loop(begin - LAG, end - LAG, pass_on, 0)

        j = s - LAG

        @pl.when((j >= 0) & (j < STEPS) & (y == 3))
        def _():
            drain(chunk(up_band, j), right_recv.at[j])

            @pl.when(j < BY_ONE)
            def _():
                send(up_band, j, down_band, y_send.at[2], relay_recv.at[j])

            send(up_band, j, partner, core_send.at[2], core_recv.at[2, place(j)[0]])
            drain(chunk(down_band, j), left_recv.at[j])
            send(down_band, j, partner, core_send.at[1], core_recv.at[1, place(j)[0]])

        @pl.when(y >= 2)
        def _():
            lax.fori_loop(begin - relay, end - relay, take_far, 0)

        for q in range(1, YS):

            @pl.when((s < EARLY) & (y < q))
            def _():
                out_ref[s, :, :, q * WIDE : (q + 1) * WIDE] = jnp.zeros((2, ROWS, WIDE), out_ref.dtype)

        return carry

    lax.fori_loop(0, STEPS + LAG + 1, step, 0)

    other = 1 - 2 * core
    late = GROUPS - 1

    @pl.when(core == 1)
    def _():
        drain(buf.at[partner, late], core_recv.at[0, late])

    for kind, of_band, wanted in ((1, down_band, y > 0), (2, up_band, y == 3), (3, far_band, y >= 2)):

        @pl.when(wanted)
        def _():
            drain(buf.at[of_band + other, late], core_recv.at[kind, late])

    whole = buf.at[band]
    drain(buf.at[band, :, pl.ds(0, CHANS - 1)], a2a_send)

    @pl.when(core == 0)
    def _():
        drain(whole, core_send.at[0])

    @pl.when(y < 2)
    def _():
        drain(whole, y_send.at[0])

    @pl.when(y == 1)
    def _():
        drain(xs.at[pl.ds(0, STEPS - BY_ONE)], y_send.at[2])
        drain(xs.at[pl.ds(0, STEPS // 2)], y_send.at[1])

    @pl.when(mod(y, 2) == 0)
    def _():
        @pl.when(core == 0)
        def _():
            drain(chunk(band, STEPS - 3), own_send.at[STEPS - 3])

        for last in range(STEPS - 2, STEPS):
            drain(chunk(band, last), own_send.at[last])

        for last in (STEPS - 5, STEPS - 3, STEPS - 1):
            drain(chunk(band, 0), relay_send.at[last - div(y, 2)])

    @pl.when(y > 0)
    def _():
        drain(whole, core_send.at[1])

    @pl.when(y == 3)
    def _():
        drain(xs.at[pl.ds(0, BY_ONE)], y_send.at[2])
        drain(whole, core_send.at[2])

    @pl.when(y >= 2)
    def _():
        drain(whole, core_send.at[3])


def correlate(counts, exponents, spectra):
    dma = pltpu.SemaphoreType.DMA
    outs = (
        ((EARLY, 2, ROWS, BANDS * ROWS), jnp.bfloat16),
        ((BANDS, GROUPS, CHANS, GROUP, UNIT, ROWS), jnp.bfloat16),
        ((2, GROUP, 2 * ROWS, DEPTH), jnp.bfloat16),
        ((GROUP, 8, WIDE), jnp.float32),
    )
    return pl.pallas_call(
        kernel,
        out_shape=[pltpu.VMEM(*out) for out in outs],
        in_specs=[pl.BlockSpec(memory_space=pltpu.HBM)] * 3,
        out_specs=[pl.BlockSpec(memory_space=pltpu.VMEM)] * 4,
        scratch_shapes=[
            pltpu.SMEM((OWN,), jnp.int32),
            pltpu.VMEM((CHANS, UNIT, ROWS), jnp.int32),
            pltpu.VMEM((ROWS, CHANS * OWN), jnp.int32),
            pltpu.VMEM((SPANS, 2, ROWS * SAMPLES, LANES), jnp.bfloat16),
            pltpu.VMEM((2, ROWS * SAMPLES, LANES), jnp.float32),
            pltpu.VMEM((LANES * UNIT, ROWS), jnp.float32),
            pltpu.VMEM((CHANS, GROUPS, GROUP, UNIT, ROWS), jnp.bfloat16),
            dma((SPANS + 2,)),
            dma((STEPS,)), dma((STEPS,)), dma((STEPS,)), dma((STEPS,)), dma((4, GROUPS)),
            dma, dma((3,)), dma((STEPS,)), dma((STEPS,)), dma((4,)),
        ],
        compiler_params=pltpu.CompilerParams(
            collective_id=0, has_side_effects=True, vmem_limit_bytes=12 << 20
        ),
        name="correlate",
    )(*(pltpu.with_memory_space_constraint(operand, pltpu.HBM) for operand in (counts, exponents, spectra)))


def finish_kernel(early_ref, buf, forms, shares, out_ref, stage, early_sem, late_sem):
    band = lax.axis_index("band")
    copies = []
    for n in range(OUT_PARTS):
        part = pl.ds(n * (EARLY // OUT_PARTS), EARLY // OUT_PARTS)
        copies.append(pltpu.make_async_copy(early_ref.at[part], out_ref.at[part], early_sem.at[n]))
    for copy in copies:
        copy.start()
    late = GROUPS - 1
    for c in range(GROUP):
        for q in range(YS):
            columns = pl.ds(q * WIDE, WIDE)
            right = jnp.concatenate(
                [buf[2 * q, late, :, c].reshape(DEPTH, ROWS), buf[2 * q + 1, late, :, c].reshape(DEPTH, ROWS)], axis=1
            )
            product = jnp.dot(forms[late % 2, c], right, preferred_element_type=jnp.float32) * shares[c, :1]
            for part in range(2):
                tile = lower(product[part * ROWS : (part + 1) * ROWS], band * ROWS - q * WIDE)
                stage[c, part, :, columns] = tile.astype(jnp.bfloat16)

        copies.append(pltpu.make_async_copy(stage.at[c], out_ref.at[EARLY + c], late_sem.at[c]))
        copies[-1].start()
    for copy in copies:
        copy.wait()


def finish(early, buf, forms, shares):
    vmem = pl.BlockSpec(memory_space=pltpu.VMEM)
    return pl.pallas_call(
        finish_kernel,
        out_shape=jax.ShapeDtypeStruct((OWN, 2, ROWS, BANDS * ROWS), jnp.bfloat16),
        in_specs=[vmem] * 4,
        out_specs=pl.BlockSpec(memory_space=pl.ANY),
        scratch_shapes=[
            pltpu.VMEM((GROUP, 2, ROWS, BANDS * ROWS), jnp.bfloat16),
            pltpu.SemaphoreType.DMA((OUT_PARTS,)),
            pltpu.SemaphoreType.DMA((GROUP,)),
        ],
        compiler_params=pltpu.CompilerParams(vmem_limit_bytes=12 << 20),
        name="finish",
    )(*(pltpu.with_memory_space_constraint(operand, pltpu.VMEM) for operand in (early, buf, forms, shares)))


def local(spectra, exponents, counts):
    flat = jnp.transpose(spectra, (0, 1, 3, 2)).reshape(2, ROWS * SAMPLES, CHANS * OWN)
    return finish(*correlate(counts, exponents, flat))


def solution(mesh):
    placed = (P(None, "band", None, "chan"), P("band", None), P("chan"))
    return jax.shard_map(
        local, mesh=mesh, in_specs=placed, out_specs=P("chan", None, "band", None), check_vma=False
    )
```

```python
import jax
import jax.numpy as jnp
from jax import lax
from jax.experimental import pallas as pl
from jax.experimental.pallas import tpu as pltpu
from jax.sharding import PartitionSpec as P

MESH = pl.DeviceIdType.MESH
BLOCK = 64
BANDS, CORES, YS = 8, 2, 4
ZS, XS = 8, 4
CHANS = ZS * XS
ROWS = 128
OWN = 16
SAMPLES = 8
UNIT = 2 * SAMPLES
DEPTH = CHANS * UNIT
WIDE = 2 * ROWS
GROUPS = 4
GROUP = OWN // GROUPS
EARLY = OWN - GROUP
CHUNK = 4
PARTS = CHANS // CHUNK
STEPS = GROUPS * PARTS
WHOLE = 12, 17, 22, 27
DIRECT = 17, 23, 29
SECOND = 19, 25, 31
AHEAD = 16
BY_ONE = 24
LANES = 128
SPANS = CHANS * OWN // LANES
LAG = 3
NEAR = 2 * GROUPS
FEW = 28
FLIGHT = 4
OUT_PARTS = 6


def power_scale(exponents):
    scale = jnp.zeros(exponents.shape, jnp.float32)
    for power in range(-2, 3):
        scale = scale + jnp.where(exponents == power, jnp.float32(2.0**power), jnp.float32(0.0))
    return scale


def mod(a, n):
    return a % n if isinstance(a, int) else lax.rem(a, jnp.full_like(a, n))


def div(a, n):
    return a // n if isinstance(a, int) else lax.div(a, jnp.full_like(a, n))


def flip(a, b, bits):
    return sum(mod(div(a, 1 << n) + div(b, 1 << n), 2) * (1 << n) for n in range(bits))


def far_first(n):
    return 2 * mod(n, 2) + div(n, 2)


def offset(k):
    return 2 * far_first(div(k, 2 * CHUNK)) + mod(k, 2), div(mod(k, CHUNK), 2) + 2 * mod(div(k, CHUNK), 2)


def place(s):
    near = int(s < NEAR) if isinstance(s, int) else (s < NEAR).astype(jnp.int32)
    rest = s - NEAR
    group = near * div(s, 2) + (1 - near) * div(rest, PARTS - 2)
    return group, near * mod(s, 2) + (1 - near) * (2 + mod(rest, PARTS - 2))


def source(chan, k):
    dz, dx = offset(k)
    return flip(div(chan, XS), dz, 3) * XS + mod(mod(chan, XS) + dx, XS)


def target(chan, k):
    dz, dx = offset(k)
    return flip(div(chan, XS), dz, 3) * XS + mod(mod(chan, XS) + XS - dx, XS)


def lower(tile, first):
    line = lax.broadcasted_iota(jnp.int32, tile.shape, 0)
    column = lax.broadcasted_iota(jnp.int32, tile.shape, 1)
    limit = jnp.where(line < BLOCK, BLOCK, 2 * BLOCK) + first
    return jnp.where(column < limit, tile, 0.0)


def kernel(
    counts_hbm, exponents_ref, x_ref, out_ref, buf, forms, shares, counts_ref, times, powers, raw, wide, narrow, xs, load_sem,
    a2a_recv, left_recv, right_recv, relay_recv, core_recv, a2a_send, y_send, own_send, relay_send, core_send,
):
    band = lax.axis_index("band")
    chan = lax.axis_index("chan")
    y, core = div(band, CORES), mod(band, CORES)
    partner = band + 1 - 2 * core
    up, down, far = mod(y + 1, YS), mod(y + YS - 1, YS), mod(y + 2, YS)
    slow = (y == 2).astype(jnp.int32)
    relay = 9 + 3 * slow
    due_far = 20 + slow, 24 + 2 * slow, 30 + slow
    up_band, down_band, far_band = up * CORES + core, down * CORES + core, far * CORES + core

    barrier = pltpu.get_barrier_semaphore()

    def greet(k, carry):
        pl.semaphore_signal(barrier, inc=1, device_id=(band, target(chan, k)), device_id_type=MESH)
        return carry

    def drain(ref, sem):
        pltpu.make_async_copy(ref, ref, sem).wait()

    def span(n):
        return flip(div(chan, 2 * XS), far_first(n), 2)

    def lanes(n):
        return pl.ds(pl.multiple_of(span(n) * LANES, LANES), LANES)

    loads = [
        pltpu.make_async_copy(exponents_ref, powers, load_sem.at[SPANS]),
        pltpu.make_async_copy(counts_hbm, counts_ref, load_sem.at[SPANS + 1]),
    ] + [pltpu.make_async_copy(x_ref.at[:, :, lanes(n)], raw.at[n], load_sem.at[n]) for n in range(SPANS)]
    for load in loads:
        load.start()

    for other in (up_band, down_band, partner):
        pl.semaphore_signal(barrier, inc=1, device_id=(other, chan), device_id_type=MESH)
    lax.fori_loop(1, CHANS, greet, 0)

    def turn(n):
        drain(raw.at[n], load_sem.at[n])
        scale = power_scale(powers[:, lanes(n)])
        for part in range(2):
            wide[part] = raw[n, part].astype(jnp.float32)
            for t in range(SAMPLES):
                tile = wide[part, pl.ds(t, ROWS, stride=SAMPLES), :] * scale
                narrow[pl.ds(part * SAMPLES + t, LANES, stride=UNIT), :] = tile.T

        def pack(d, carry):
            own = narrow[pl.ds(pl.multiple_of(d * (OWN * UNIT), OWN * UNIT), OWN * UNIT), :]
            xs[span(n) * (LANES // OWN) + d] = own.astype(jnp.bfloat16).reshape(GROUPS, GROUP, UNIT, ROWS)
            return carry

        lax.fori_loop(0, LANES // OWN, pack, 0)

    loads[0].wait()
    turn(0)
    for g in range(GROUPS):
        pltpu.make_async_copy(xs.at[chan, g], buf.at[band, g, 0], a2a_recv.at[2 * g]).start()

    pl.semaphore_wait(barrier, CHANS + 2)

    def scatter(s):
        g, part = place(s)

        for n in range(CHUNK):
            k = part * CHUNK + n
            to = target(chan, k)

            @pl.when(k > 0)
            def _():
                pltpu.make_async_remote_copy(
                    src_ref=xs.at[to, g], dst_ref=buf.at[band, g, k],
                    send_sem=a2a_send, recv_sem=a2a_recv.at[s],
                    device_id=(band, to), device_id_type=MESH,
                ).start()

    def scatter_all(first, end):
        def one(s, carry):
            scatter(s)
            return carry

        lax.fori_loop(first, end, one, 0)

    scatter_all(0, NEAR // 2)
    turn(1)
    scatter_all(NEAR, NEAR + 2)

    piece = lax.broadcasted_iota(jnp.int32, times.shape, 0)
    row = lax.broadcasted_iota(jnp.int32, times.shape, 1)
    times[...] = source(chan, piece) * SAMPLES + mod(row, SAMPLES)
    loads[1].wait()
    for c in range(GROUP):
        shares[c] = 1.0 / jnp.full(shares.shape[1:], counts_ref[EARLY + c], jnp.int32).astype(jnp.float32)

    def chunk(of_band, s):
        g, part = place(s)
        return buf.at[of_band, g, pl.ds(part * CHUNK, CHUNK)]

    def send(of_band, s, to_band, send_sem, recv_sem):
        ref = chunk(of_band, s)
        pltpu.make_async_remote_copy(
            src_ref=ref, dst_ref=ref, send_sem=send_sem, recv_sem=recv_sem,
            device_id=(to_band, chan), device_id_type=MESH,
        ).start()

    def prepare(g, c):
        slot = mod(g, 2)
        own = buf[band, g, :, c].astype(jnp.float32)
        own = jnp.where(times[...] < counts_ref[g * GROUP + c], own, 0.0)
        swapped = jnp.concatenate([own[:, SAMPLES:], -own[:, :SAMPLES]], axis=1)
        forms[slot, c, :ROWS] = own.astype(jnp.bfloat16).reshape(DEPTH, ROWS).T
        forms[slot, c, ROWS:] = swapped.astype(jnp.bfloat16).reshape(DEPTH, ROWS).T

    def gram(g, q, diagonal):
        slot = mod(g, 2)
        columns = pl.ds(pl.multiple_of(q * WIDE, WIDE), WIDE)

        for c in range(GROUP):
            right = jnp.concatenate(
                [buf[2 * q, g, :, c].reshape(DEPTH, ROWS), buf[2 * q + 1, g, :, c].reshape(DEPTH, ROWS)], axis=1
            )
            share = 1.0 / jnp.full((1, WIDE), counts_ref[g * GROUP + c], jnp.int32).astype(jnp.float32)
            product = jnp.dot(forms[slot, c], right, preferred_element_type=jnp.float32) * share
            for part in range(2):
                tile = product[part * ROWS : (part + 1) * ROWS]
                if diagonal:
                    tile = lower(tile, core * ROWS)
                out_ref[g * GROUP + c, part, :, columns] = tile.astype(jnp.bfloat16)

    def front(s, carry):
        @pl.when(s < STEPS)
        def _():
            drain(chunk(band, s), a2a_recv.at[s])

            @pl.when(y < 2)
            def _():
                send(band, s, up_band, y_send.at[0], left_recv.at[s])

            @pl.when((y == 1) & (mod(s, 2) == 1))
            def _():
                send(band, s, down_band, y_send.at[1], right_recv.at[s])

            @pl.when(core == 0)
            def _():
                send(band, s, partner, core_send.at[0], core_recv.at[0, place(s)[0]])

        @pl.when((s > 2) & (s + AHEAD < STEPS))
        def _():
            scatter(s + AHEAD)

        return carry

    def pass_on(j, carry):
        @pl.when((j >= 0) & (j < STEPS) & (y == 0) & (mod(j, 2) == 1))
        def _():
            drain(chunk(up_band, j), right_recv.at[j])

            @pl.when(j >= 7)
            def _():
                drain(chunk(up_band, j - 6), relay_send.at[j - 6])

            send(up_band, j, down_band, relay_send.at[j], relay_recv.at[j])

        @pl.when((j >= 0) & (j < STEPS) & (y > 0))
        def _():
            drain(chunk(down_band, j), left_recv.at[j])

            @pl.when((y == 1) & (j >= BY_ONE))
            def _():
                send(down_band, j, up_band, y_send.at[2], relay_recv.at[j])

            @pl.when((y == 2) & (mod(j, 2) == 0))
            def _():
                @pl.when(j >= 6)
                def _():
                    drain(chunk(down_band, j - 6), relay_send.at[j - 6])

                send(down_band, j, up_band, relay_send.at[j], relay_recv.at[j])

            send(down_band, j, partner, core_send.at[1], core_recv.at[1, place(j)[0]])

        return carry

    def take_far(i, carry):
        @pl.when((i >= 0) & (i < STEPS))
        def _():
            drain(chunk(far_band, i), relay_recv.at[i])
            send(far_band, i, partner, core_send.at[3], core_recv.at[3, place(i)[0]])

        return carry

    def step(s, carry):
        def due(steps):
            ready = (s == steps[0]) | (s == steps[1]) | (s == steps[2])
            return ready, (s >= steps[1]).astype(jnp.int32) + (s >= steps[2]).astype(jnp.int32)

        other = 1 - 2 * core

        begun = [s >= first for first in WHOLE]
        g1 = sum(one.astype(jnp.int32) for one in begun) - 1
        since = s - WHOLE[0]
        for one, first, last in zip(begun[1:], WHOLE[1:], WHOLE[:-1]):
            since = since - one.astype(jnp.int32) * (first - last)

        @pl.when((since >= 0) & (since < GROUP))
        def _():
            prepare(g1, since)

        @pl.when((since == GROUP) & (g1 < GROUPS - 1))
        def _():
            @pl.when(core == 1)
            def _():
                drain(buf.at[partner, g1], core_recv.at[0, g1])

            gram(g1, y, True)

        ready, g2 = due(DIRECT)

        @pl.when(ready & (y > 0))
        def _():
            drain(buf.at[down_band + other, g2], core_recv.at[1, g2])
            gram(g2, down, False)

        ready, g3 = due(SECOND)

        @pl.when(ready & (y == 3))
        def _():
            drain(buf.at[up_band + other, g3], core_recv.at[2, g3])
            gram(g3, up, False)

        ready, g4 = due(due_far)

        @pl.when(ready & (y >= 2))
        def _():
            drain(buf.at[far_band + other, g4], core_recv.at[3, g4])
            gram(g4, far, False)

        begin, end = s + div(s - 1, 4), s + div(s, 4) + 1
        lax.fori_loop(begin, end, front, 0)

        @pl.when((s < STEPS) & (mod(y, 2) == 0))
        def _():
            flight = FLIGHT - core

            @pl.when((s >= flight) & (s <= FEW))
            def _():
                drain(chunk(band, s - flight), own_send.at[s - flight])

            @pl.when(s >= FEW)
            def _():
                drain(chunk(band, s - flight + 1), own_send.at[s - flight + 1])

            @pl.when(y == 2)
            def _():
                send(band, s, up_band, own_send.at[s], left_recv.at[s])

            @pl.when(y == 0)
            def _():
                send(band, s, down_band, own_send.at[s], right_recv.at[s])

        @pl.when(s == 0)
        def _():
            scatter_all(NEAR // 2, NEAR)

        @pl.when(s < SPANS - 2)
        def _():
            turn(s + 2)
            scatter_all(NEAR + 2 * s + 2, NEAR + 2 * s + 4)

        @pl.when(s == SPANS - 3)
        def _():
            scatter_all(NEAR + 2 * SPANS - 2, AHEAD + 3)

        @pl.when(y < 3)
        def _():
            lax.fori_loop(begin - LAG, end - LAG, pass_on, 0)

        j = s - LAG

        @pl.when((j >= 0) & (j < STEPS) & (y == 3))
        def _():
            drain(chunk(up_band, j), right_recv.at[j])

            @pl.when(j < BY_ONE)
            def _():
                send(up_band, j, down_band, y_send.at[2], relay_recv.at[j])

            send(up_band, j, partner, core_send.at[2], core_recv.at[2, place(j)[0]])
            drain(chunk(down_band, j), left_recv.at[j])
            send(down_band, j, partner, core_send.at[1], core_recv.at[1, place(j)[0]])

        @pl.when(y >= 2)
        def _():
            lax.fori_loop(begin - relay, end - relay, take_far, 0)

        for q in range(1, YS):

            @pl.when((s < EARLY) & (y < q))
            def _():
                out_ref[s, :, :, q * WIDE : (q + 1) * WIDE] = jnp.zeros((2, ROWS, WIDE), out_ref.dtype)

        return carry

    lax.fori_loop(0, STEPS + LAG + 1, step, 0)

    other = 1 - 2 * core
    late = GROUPS - 1

    @pl.when(core == 1)
    def _():
        drain(buf.at[partner, late], core_recv.at[0, late])

    for kind, of_band, wanted in ((1, down_band, y > 0), (2, up_band, y == 3), (3, far_band, y >= 2)):

        @pl.when(wanted)
        def _():
            drain(buf.at[of_band + other, late], core_recv.at[kind, late])

    whole = buf.at[band]
    drain(buf.at[band, :, pl.ds(0, CHANS - 1)], a2a_send)

    @pl.when(core == 0)
    def _():
        drain(whole, core_send.at[0])

    @pl.when(y < 2)
    def _():
        drain(whole, y_send.at[0])

    @pl.when(y == 1)
    def _():
        drain(xs.at[pl.ds(0, STEPS - BY_ONE)], y_send.at[2])
        drain(xs.at[pl.ds(0, STEPS // 2)], y_send.at[1])

    @pl.when(mod(y, 2) == 0)
    def _():
        @pl.when(core == 0)
        def _():
            drain(chunk(band, STEPS - 3), own_send.at[STEPS - 3])

        for last in range(STEPS - 2, STEPS):
            drain(chunk(band, last), own_send.at[last])

        for last in (STEPS - 5, STEPS - 3, STEPS - 1):
            drain(chunk(band, 0), relay_send.at[last - div(y, 2)])

    @pl.when(y > 0)
    def _():
        drain(whole, core_send.at[1])

    @pl.when(y == 3)
    def _():
        drain(xs.at[pl.ds(0, BY_ONE)], y_send.at[2])
        drain(whole, core_send.at[2])

    @pl.when(y >= 2)
    def _():
        drain(whole, core_send.at[3])


def correlate(counts, exponents, spectra):
    dma = pltpu.SemaphoreType.DMA
    outs = (
        ((EARLY, 2, ROWS, BANDS * ROWS), jnp.bfloat16),
        ((BANDS, GROUPS, CHANS, GROUP, UNIT, ROWS), jnp.bfloat16),
        ((2, GROUP, 2 * ROWS, DEPTH), jnp.bfloat16),
        ((GROUP, 8, WIDE), jnp.float32),
    )
    return pl.pallas_call(
        kernel,
        out_shape=[pltpu.VMEM(*out) for out in outs],
        in_specs=[pl.BlockSpec(memory_space=pltpu.HBM)] * 3,
        out_specs=[pl.BlockSpec(memory_space=pltpu.VMEM)] * 4,
        scratch_shapes=[
            pltpu.SMEM((OWN,), jnp.int32),
            pltpu.VMEM((CHANS, UNIT, ROWS), jnp.int32),
            pltpu.VMEM((ROWS, CHANS * OWN), jnp.int32),
            pltpu.VMEM((SPANS, 2, ROWS * SAMPLES, LANES), jnp.bfloat16),
            pltpu.VMEM((2, ROWS * SAMPLES, LANES), jnp.float32),
            pltpu.VMEM((LANES * UNIT, ROWS), jnp.float32),
            pltpu.VMEM((CHANS, GROUPS, GROUP, UNIT, ROWS), jnp.bfloat16),
            dma((SPANS + 2,)),
            dma((STEPS,)), dma((STEPS,)), dma((STEPS,)), dma((STEPS,)), dma((4, GROUPS)),
            dma, dma((3,)), dma((STEPS,)), dma((STEPS,)), dma((4,)),
        ],
        compiler_params=pltpu.CompilerParams(
            collective_id=0, has_side_effects=True, vmem_limit_bytes=12 << 20
        ),
        name="correlate",
    )(*(pltpu.with_memory_space_constraint(operand, pltpu.HBM) for operand in (counts, exponents, spectra)))


def finish_kernel(early_ref, buf, forms, shares, out_ref, stage, early_sem, late_sem):
    band = lax.axis_index("band")
    copies = []
    for n in range(OUT_PARTS):
        part = pl.ds(n * (EARLY // OUT_PARTS), EARLY // OUT_PARTS)
        copies.append(pltpu.make_async_copy(early_ref.at[part], out_ref.at[part], early_sem.at[n]))
    for copy in copies:
        copy.start()
    late = GROUPS - 1
    for c in range(GROUP):
        for q in range(YS):
            columns = pl.ds(q * WIDE, WIDE)
            right = jnp.concatenate(
                [buf[2 * q, late, :, c].reshape(DEPTH, ROWS), buf[2 * q + 1, late, :, c].reshape(DEPTH, ROWS)], axis=1
            )
            product = jnp.dot(forms[late % 2, c], right, preferred_element_type=jnp.float32) * shares[c, :1]
            for part in range(2):
                tile = lower(product[part * ROWS : (part + 1) * ROWS], band * ROWS - q * WIDE)
                stage[c, part, :, columns] = tile.astype(jnp.bfloat16)

        copies.append(pltpu.make_async_copy(stage.at[c], out_ref.at[EARLY + c], late_sem.at[c]))
        copies[-1].start()
    for copy in copies:
        copy.wait()


def finish(early, buf, forms, shares):
    vmem = pl.BlockSpec(memory_space=pltpu.VMEM)
    return pl.pallas_call(
        finish_kernel,
        out_shape=jax.ShapeDtypeStruct((OWN, 2, ROWS, BANDS * ROWS), jnp.bfloat16),
        in_specs=[vmem] * 4,
        out_specs=pl.BlockSpec(memory_space=pl.ANY),
        scratch_shapes=[
            pltpu.VMEM((GROUP, 2, ROWS, BANDS * ROWS), jnp.bfloat16),
            pltpu.SemaphoreType.DMA((OUT_PARTS,)),
            pltpu.SemaphoreType.DMA((GROUP,)),
        ],
        compiler_params=pltpu.CompilerParams(vmem_limit_bytes=12 << 20),
        name="finish",
    )(*(pltpu.with_memory_space_constraint(operand, pltpu.VMEM) for operand in (early, buf, forms, shares)))


def local(spectra, exponents, counts):
    flat = jnp.transpose(spectra, (0, 1, 3, 2)).reshape(2, ROWS * SAMPLES, CHANS * OWN)
    return finish(*correlate(counts, exponents, flat))


def solution(mesh):
    placed = (P(None, "band", None, "chan"), P("band", None), P("chan"))
    return jax.shard_map(
        local, mesh=mesh, in_specs=placed, out_specs=P("chan", None, "band", None), check_vma=False
    )
```
